256 devices in a mesh: dcn: 4 (over x), fsdp: 16 (over y, z_lo), tp: 4 (over z_hi, core).
Axes of the slice: x: 4, y: 4, z: 8 (z_hi: 2, z_lo: 4; z = z_hi * 4 + z_lo), core: 2. Of those that a mesh axis runs over, the one named last changes fastest.
Arguments:
- inputs: bfloat16 [320, 4608], P(None, 'dcn'), may hold values from -6 to 6
- target: bfloat16 [320, 4608], P(None, 'dcn'), may hold values from -6 to 6
- w_gate: bfloat16 [4608, 18432], P(('dcn', 'fsdp'), 'tp'), may hold values from -0.09375 to 0.09375
- w_up: bfloat16 [4608, 18432], P(('dcn', 'fsdp'), 'tp'), may hold values from -0.09375 to 0.09375
- w_down: bfloat16 [18432, 4608], P('tp', ('dcn', 'fsdp')), may hold values from -0.046875 to 0.046875
- start_gate: bfloat16 [4608, 18432], P(('dcn', 'fsdp'), 'tp'), may hold values from -350 to 350
- start_up: bfloat16 [4608, 18432], P(('dcn', 'fsdp'), 'tp'), may hold values from -350 to 350
- start_down: bfloat16 [18432, 4608], P('tp', ('dcn', 'fsdp')), may hold values from -350 to 350
Outputs:
- next_gate: float32 [4608, 4, 4608], P('dcn', 'tp', 'fsdp')
- next_up: float32 [4608, 4, 4608], P('dcn', 'tp', 'fsdp')
- next_down: float32 [4, 4608, 4608], P('tp', 'fsdp', 'dcn')
- hessenberg: float32 [4], replicated
- rayleigh: float32 [1], replicated
The draws below stay inside these ranges and needn't reach their ends.
All inputs are finite; a program needn't handle non-finite values.
Results may differ from the reference program's by a relative error of at most 0.014.
Values may be sent and summed in bfloat16 or wider, within the bound.
A program may use at most 64 MiB of HBM per device.

```python
import math
import jax
import jax.numpy as jnp

D = 4608
FF = 18432
TOKENS = 320
N_TP = 4


def unit_levels(key):
    order = jax.random.permutation(jax.random.fold_in(key, 5), 64)
    block = jnp.arange(FF, dtype=jnp.int32) * 64 // FF
    ranks = order[block].astype(jnp.float32)
    return jnp.power(jnp.float32(10.0), -4.0 * ranks / 63.0)


def spread_scales(key, rows, cols, spread):
    row_key, col_key = jax.random.split(key)
    row_scale = jnp.exp(jax.random.uniform(row_key, (rows, 1), jnp.float32) * math.log(spread))
    col_scale = jnp.exp(jax.random.uniform(col_key, (1, cols), jnp.float32) * math.log(spread))
    return row_scale * col_scale


def draw_start_gate(key, part):
    levels = unit_levels(key)
    key = jax.random.fold_in(key, 11)
    scale_key, base_key = jax.random.split(key)
    scales = spread_scales(scale_key, D, FF, 10.0) * levels[None, :]
    base = jnp.clip(jax.random.normal(base_key, (D, FF), jnp.float32), -3.5, 3.5)
    return (base * scales).astype(jnp.bfloat16)


def draw_start_up(key, part):
    levels = unit_levels(key)
    key = jax.random.fold_in(key, 23)
    scale_key, base_key = jax.random.split(key)
    scales = spread_scales(scale_key, D, FF, 10.0) * levels[None, :]
    base = jnp.clip(jax.random.normal(base_key, (D, FF), jnp.float32), -3.5, 3.5)
    return (base * scales).astype(jnp.bfloat16)


def draw_start_down(key, part):
    levels = unit_levels(key)
    key = jax.random.fold_in(key, 37)
    scale_key, base_key = jax.random.split(key)
    scales = spread_scales(scale_key, FF, D, 10.0) * levels[:, None]
    base = jnp.clip(jax.random.normal(base_key, (FF, D), jnp.float32), -3.5, 3.5)
    return (base * scales).astype(jnp.bfloat16)


def shard_levels(rng, dims, pieces, low, high):
    factor_of = 1.0
    for position, shards_of in pieces:
        steps = jax.random.uniform(jax.random.fold_in(jax.random.fold_in(rng, 6), position), (shards_of,), jnp.float32, low / len(pieces), high / len(pieces))
        factor_of = factor_of * jnp.repeat(jnp.exp(steps), dims[position] // shards_of).reshape((-1,) + (1,) * (len(dims) - 1 - position))
    return factor_of


def scatter_about(key, dims, scale, most, pieces=(), held_as=jnp.bfloat16):
    result = scale * jax.random.normal(key, dims, jnp.float32)
    if pieces:
        result = result * shard_levels(key, dims, pieces, -0.22, 0.18)
    return jnp.clip(result, -most, most).astype(held_as)


def setup_inputs(seed: int = 0) -> dict:
    key_list = jax.random.split(jax.random.key(seed), 9)
    inputs = scatter_about(key_list[0], (TOKENS, D), 1.0, 6.0, ((1, 4),))
    target = scatter_about(key_list[1], (TOKENS, D), 1.0, 6.0, ((1, 4),))
    w_gate = scatter_about(key_list[2], (D, FF), D ** -0.5, 0.09375, ((0, 64), (1, 4)))
    w_up = scatter_about(key_list[3], (D, FF), D ** -0.5, 0.09375, ((0, 64), (1, 4)))
    w_down = scatter_about(key_list[4], (FF, D), FF ** -0.5, 0.046875, ((0, 4), (1, 64)))
    start_gate = draw_start_gate(jax.random.fold_in(key_list[8], 71), 0)
    start_up = draw_start_up(jax.random.fold_in(key_list[8], 71), 0)
    start_down = draw_start_down(jax.random.fold_in(key_list[8], 71), 0)
    return {"inputs": inputs, "target": target, "w_gate": w_gate, "w_up": w_up, "w_down": w_down, "start_gate": start_gate, "start_up": start_up, "start_down": start_down}


gelu_cubic = 0.044715
gelu_scale = math.sqrt(2.0 / math.pi)
epsilon = 1e-06

def gelu_parts(argument):
    squared = argument * argument
    inner_arg = gelu_scale * (argument + gelu_cubic * squared * argument)
    tanh_val = jnp.tanh(inner_arg)
    sech_square = 1.0 - tanh_val * tanh_val
    inner_slope = gelu_scale * (1.0 + 3.0 * gelu_cubic * squared)
    inner_curve = gelu_scale * 6.0 * gelu_cubic * argument
    gelu_val = 0.5 * argument * (1.0 + tanh_val)
    gelu_slope = 0.5 * (1.0 + tanh_val) + 0.5 * argument * sech_square * inner_slope
    gelu_curve = sech_square * inner_slope + 0.5 * argument * (sech_square * inner_curve - 2.0 * tanh_val * sech_square * inner_slope * inner_slope)
    return (gelu_val, gelu_slope, gelu_curve)

def product(former, latter):
    return jnp.dot(former, latter, preferred_element_type=jnp.float32)

def inner(former, latter):
    entries = jnp.float32(3 * D * FF)
    total_sum = jnp.sum(former[0] * latter[0]) + jnp.sum(former[1] * latter[1]) + jnp.sum(former[2] * latter[2])
    return total_sum / entries

def reference(inputs, target, w_gate, w_up, w_down, start_gate, start_up, start_down):
    gate_pre = product(inputs, w_gate)
    up_pre = product(inputs, w_up)
    gelu_val, gelu_slope, gelu_curve = gelu_parts(gate_pre)
    hidden = (gelu_val * up_pre).astype(jnp.bfloat16)
    output = product(hidden, w_down)
    grad_out = ((output - target.astype(jnp.float32)) / TOKENS).astype(jnp.bfloat16)
    grad_hidden = product(grad_out, w_down.T)

    def hessian_apply(vector):
        tan_gate = vector[0].astype(jnp.bfloat16)
        tan_up = vector[1].astype(jnp.bfloat16)
        tan_down = vector[2].astype(jnp.bfloat16)
        gate_dot = product(inputs, tan_gate)
        up_dot = product(inputs, tan_up)
        hidden_dot = (gelu_slope * gate_dot * up_pre + gelu_val * up_dot).astype(jnp.bfloat16)
        grad_dot = ((product(hidden_dot, w_down) + product(hidden, tan_down)) / TOKENS).astype(jnp.bfloat16)
        back_dot = product(grad_dot, w_down.T) + product(grad_out, tan_down.T)
        gate_term = (back_dot * up_pre * gelu_slope + grad_hidden * up_dot * gelu_slope + grad_hidden * up_pre * gelu_curve * gate_dot).astype(jnp.bfloat16)
        up_term = (back_dot * gelu_val + grad_hidden * gelu_slope * gate_dot).astype(jnp.bfloat16)
        return (product(inputs.T, gate_term), product(inputs.T, up_term), product(hidden_dot.T, grad_out) + product(hidden.T, grad_dot))
    start_vec = (start_gate.astype(jnp.float32), start_up.astype(jnp.float32), start_down.astype(jnp.float32))
    image_one = hessian_apply(start_vec)
    factor = 1.0 / jnp.sqrt(inner(start_vec, start_vec) + epsilon)
    basis_one = tuple((member * factor for member in start_vec))
    applied = tuple((member * factor for member in image_one))
    arnoldi_11 = inner(basis_one, applied)
    residual = tuple((later - arnoldi_11 * earlier for later, earlier in zip(applied, basis_one)))
    arnoldi_21 = jnp.sqrt(inner(residual, residual) + epsilon)
    basis_two = tuple((member / arnoldi_21 for member in residual))
    image_two = hessian_apply(basis_two)
    arnoldi_12 = inner(basis_one, image_two)
    arnoldi_22 = inner(basis_two, image_two)
    residual = tuple((later - arnoldi_12 * first_vec - arnoldi_22 * second_vec for later, first_vec, second_vec in zip(image_two, basis_one, basis_two)))
    arnoldi_32 = jnp.sqrt(inner(residual, residual) + epsilon)
    basis_three = tuple((member / arnoldi_32 for member in residual))
    next_gate = basis_three[0].reshape(D, N_TP, FF // N_TP)
    next_up = basis_three[1].reshape(D, N_TP, FF // N_TP)
    next_down = basis_three[2].reshape(N_TP, FF // N_TP, D)
    hessenberg = jnp.stack([arnoldi_21, arnoldi_12, arnoldi_22, arnoldi_32]).astype(jnp.float32)
    rayleigh = jnp.stack([arnoldi_11]).astype(jnp.float32)
    return (next_gate, next_up, next_down, hessenberg, rayleigh)
```

```python
import math

import jax
import jax.numpy as jnp
from jax import lax
from jax.experimental import pallas as pl
from jax.experimental.pallas import tpu as pltpu
from jax.sharding import PartitionSpec as P

D = 4608
FF = 18432
TOK = 320
DB = 1152
HB = 288
TQ = 80
RQ = 16
NRED = 5
LO = 640
LS = 512
BLK = 144
ENTRIES = float(3 * D * FF)
EPS = 1e-06
SCALE = 2.0**-14
MESH = pl.DeviceIdType.MESH
BF = jnp.bfloat16
F32 = jnp.float32

gelu_cubic = 0.044715
gelu_scale = math.sqrt(2.0 / math.pi)


def gelu_parts(argument):
    squared = argument * argument
    inner_arg = gelu_scale * (argument + gelu_cubic * squared * argument)
    tanh_val = jnp.tanh(inner_arg)
    sech_square = 1.0 - tanh_val * tanh_val
    inner_slope = gelu_scale * (1.0 + 3.0 * gelu_cubic * squared)
    inner_curve = gelu_scale * 6.0 * gelu_cubic * argument
    gelu_val = 0.5 * argument * (1.0 + tanh_val)
    gelu_slope = 0.5 * (1.0 + tanh_val) + 0.5 * argument * sech_square * inner_slope
    gelu_curve = sech_square * inner_slope + 0.5 * argument * (
        sech_square * inner_curve - 2.0 * tanh_val * sech_square * inner_slope * inner_slope
    )
    return (gelu_val, gelu_slope, gelu_curve)


def nn(a, b):
    return lax.dot_general(a, b, (((1,), (0,)), ((), ())), preferred_element_type=F32)


def nt(a, b):
    return lax.dot_general(a, b, (((1,), (1,)), ((), ())), preferred_element_type=F32)


def tn(a, b):
    return lax.dot_general(a, b, (((0,), (0,)), ((), ())), preferred_element_type=F32)


class Place:
    def __init__(self):
        self.x = lax.axis_index("dcn")
        fsdp = lax.axis_index("fsdp")
        tp = lax.axis_index("tp")
        self.y = fsdp // 4
        self.z = (tp // 2) * 4 + fsdp % 4
        self.c = tp % 2

    def dev(self, x=None, y=None, z=None, c=None):
        x = self.x if x is None else x
        y = self.y if y is None else y
        z = self.z if z is None else z
        c = self.c if c is None else c
        return (x, y * 4 + z % 4, (z // 4) * 2 + c)

    def at_x(self, k):
        return self.dev(x=(self.x + k) % 4)

    def at_y(self, k):
        return self.dev(y=(self.y + k) % 4)

    def at_z(self, k):
        return self.dev(z=(self.z + k) % 8)

    def other(self):
        return self.dev(c=1 - self.c)


def rows_of(index, size):
    return pl.ds(pl.multiple_of(index * size, size), size)


def lanes_of(index, step, size):
    return pl.ds(pl.multiple_of(index * step, 128), size)


def remote(src, dst, ssem, rsem, dev):
    return pltpu.make_async_remote_copy(
        src_ref=src, dst_ref=dst, send_sem=ssem, recv_sem=rsem, device_id=dev, device_id_type=MESH
    )


class Flight:
    def __init__(self):
        self.sent = []

    def start(self, src, dst, ssem, rsem, dev):
        copy = remote(src, dst, ssem, rsem, dev)
        copy.start()
        self.sent.append(copy)
        return copy


def scatter_x(me, fl, stage, slots, sems):
    out = []
    for k in (1, 2, 3):
        peer = (me.x + k) % 4
        out.append(
            fl.start(
                stage.at[:, rows_of(peer, TQ), :],
                slots.at[k - 1],
                sems.at[0, k - 1],
                sems.at[1, k - 1],
                me.at_x(k),
            )
        )
    return out


def gather_x(me, fl, buf, sems):
    out = []
    mine = buf.at[:, rows_of(me.x, TQ), :]
    for k in (1, 2, 3):
        out.append(fl.start(mine, mine, sems.at[0, k - 1], sems.at[1, k - 1], me.at_x(k)))
    return out


def landed(copies):
    for copy in copies:
        copy.wait_recv()


class Reduce64:
    def __init__(self, me, fl, n, s):
        self.me, self.fl, self.n = me, fl, n
        (self.acc, self.send, self.r1, self.t1, self.t1b, self.r2, self.t2, self.t2b, self.r3, self.sems) = s

    def put(self, index, value):
        self.acc[index] = value
        self.send[index] = value.astype(BF)

    def cores(self):
        me = self.me
        self.c1 = self.fl.start(
            self.send.at[:, :, lanes_of(1 - me.c, LS, LO)],
            self.r1,
            self.sems.at[0, 0],
            self.sems.at[1, 0],
            me.other(),
        )

    def ys(self):
        me = self.me
        self.c1.wait_recv()
        for i in range(self.n):
            total = self.acc[i, :, lanes_of(me.c, LS, LO)] + self.r1[i].astype(F32)
            self.t1[i] = total
            self.t1b[i] = total.astype(BF)
        self.c2 = []
        for k in (1, 2, 3):
            peer = (me.y + k) % 4
            self.c2.append(
                self.fl.start(
                    self.t1b.at[:, rows_of(peer, TQ), :],
                    self.r2.at[k - 1],
                    self.sems.at[0, k],
                    self.sems.at[1, k],
                    me.at_y(k),
                )
            )

    def zs(self):
        me = self.me
        landed(self.c2)
        for i in range(self.n):
            total = self.t1[i, rows_of(me.y, TQ), :]
            for k in range(3):
                total = total + self.r2[k, i].astype(F32)
            self.t2b[i] = total.astype(BF)
        for q in range(NRED):

            @pl.when(me.z != q)
            def _():
                remote(
                    self.t2b.at[:, q * RQ : (q + 1) * RQ, :],
                    self.r3.at[me.z],
                    self.sems.at[0, 4 + q],
                    self.sems.at[1, 4 + me.z],
                    me.dev(z=q),
                ).start()

    def finish(self, final, post):
        me = self.me
        mine = lanes_of(me.c, LS, LO)

        @pl.when(me.z < NRED)
        def _():
            self.r3[me.z] = self.t2b[:, rows_of(me.z, RQ), :]
            for s in range(8):

                @pl.when(me.z != s)
                def _():
                    remote(
                        self.t2b.at[:, 0:RQ, :],
                        self.r3.at[s],
                        self.sems.at[0, 4],
                        self.sems.at[1, 4 + s],
                        me.other(),
                    ).wait_recv()

            rows = pl.ds(pl.multiple_of(me.y * TQ + me.z * RQ, RQ), RQ)
            for i in range(self.n):
                total = self.r3[0, i].astype(F32)
                for s in range(1, 8):
                    total = total + self.r3[s, i].astype(F32)
                final[i, rows, mine] = post(i, total, rows, mine)
            for k in range(1, 8):
                piece = final.at[:, rows, mine]
                remote(piece, piece, self.sems.at[0, 11 + k], self.sems.at[1, 12 + me.z], me.at_z(k)).start()

        for q in range(NRED):
            piece = final.at[:, pl.ds(pl.multiple_of(me.y * TQ + q * RQ, RQ), RQ), mine]

            @pl.when(me.z != q)
            def _():
                remote(piece, piece, self.sems.at[0, 4], self.sems.at[1, 12 + q], me.other()).wait_recv()

        block = final.at[:, rows_of(me.y, TQ), mine]
        c5 = []
        for k in (1, 2, 3):
            c5.append(
                self.fl.start(block, block, self.sems.at[0, 19 + k], self.sems.at[1, 19 + k], me.at_y(k))
            )
        landed(c5)
        half = final.at[:, :, lanes_of(me.c, LO, LS)]
        c6 = self.fl.start(half, half, self.sems.at[0, 23], self.sems.at[1, 23], me.other())
        c6.wait_recv()

    def drain(self):
        me = self.me
        for q in range(NRED):

            @pl.when(me.z != q)
            def _():
                remote(
                    self.t2b.at[:, q * RQ : (q + 1) * RQ, :],
                    self.r3.at[me.z],
                    self.sems.at[0, 4 + q],
                    self.sems.at[1, 4 + me.z],
                    me.dev(z=q),
                ).wait_send()

        @pl.when(me.z < NRED)
        def _():
            for k in range(1, 8):
                remote(
                    self.t2b.at[:, 0:RQ, :],
                    self.t2b.at[:, 0:RQ, :],
                    self.sems.at[0, 11 + k],
                    self.sems.at[1, 12],
                    me.other(),
                ).wait_send()


def reduce_scratch(n):
    return [
        pltpu.VMEM((n, TOK, DB), F32),
        pltpu.VMEM((n, TOK, DB), BF),
        pltpu.VMEM((n, TOK, LO), BF),
        pltpu.VMEM((n, TOK, LO), F32),
        pltpu.VMEM((n, TOK, LO), BF),
        pltpu.VMEM((3, n, TQ, LO), BF),
        pltpu.VMEM((n, TQ, LO), F32),
        pltpu.VMEM((n, TQ, LO), BF),
        pltpu.VMEM((8, n, RQ, LO), BF),
        pltpu.SemaphoreType.DMA((2, 24)),
    ]


class ScalarSum:
    def __init__(self, me, fl, buf, sems):
        self.me, self.fl, self.buf, self.sems = me, fl, buf, sems

    def go(self, stage, tile):
        me = self.me
        count, index, base, at = (
            (2, me.c, 0, lambda k: me.other()),
            (4, me.x, 2, me.at_x),
            (4, me.y, 6, me.at_y),
            (8, me.z, 10, me.at_z),
        )[stage]
        mine = self.buf.at[base + index]
        self.buf[base + index] = tile
        self.copies = []
        for k in range(1, count):
            self.copies.append(
                self.fl.start(mine, mine, self.sems.at[0, base + k], self.sems.at[1, base + k], at(k))
            )
        self.span = (base, count)

    def get(self):
        landed(self.copies)
        base, count = self.span
        total = self.buf[base]
        for s in range(1, count):
            total = total + self.buf[base + s]
        return total


def rsqrt_of(value):
    return 1.0 / jnp.sqrt(value)


def whole_sum(value):
    return jnp.sum(jnp.sum(value, axis=1, keepdims=True), axis=0, keepdims=True)


def fold(value):
    return jnp.sum(value.reshape(BLK // 8, 8, HB), axis=0)


def tile_of(values):
    rows = [jnp.broadcast_to(v, (1, 128)) for v in values]
    while len(rows) < 8:
        rows.append(jnp.zeros((1, 128), F32))
    return jnp.concatenate(rows, axis=0)


def kernel(
    x, x_t, target, w_gate, w_up, w_down, s_gate, s_up, s_down,
    one, two, scal,
    kp, kr, kpair, sems_k,
    acc_a, send_a, slots_a, sems_a,
    own, hh, sems_h, mm, sems_m,
    red_b0, red_b1, red_b2, red_b3, red_b4, red_b5, red_b6, red_b7, red_b8, red_b9,
    gg,
    acc_c, send_c, slots_c, sems_c,
    gu1, sems_g1, u1d, tan2, h2,
    red_e0, red_e1, red_e2, red_e3, red_e4, red_e5, red_e6, red_e7, red_e8, red_e9,
    g2,
    acc_f, send_f, slots_f, sems_f,
    gu2, sems_g2,
    sbuf1, ssem1, sbuf2, ssem2,
):
    me = Place()
    fl = Flight()
    starts = (s_gate, s_up, s_down)

    barrier = pltpu.get_barrier_semaphore()
    peers = (
        [me.at_x(k) for k in (1, 2, 3)]
        + [me.at_y(k) for k in (1, 2, 3)]
        + [me.at_z(k) for k in range(1, 8)]
        + [me.other()]
    )
    for peer in peers:
        pl.semaphore_signal(barrier, inc=1, device_id=peer, device_id_type=MESH)

    for i, w in enumerate((w_gate, w_up, s_gate, s_up)):
        part = nn(x[...], w[...])
        acc_a[i] = part
        send_a[i] = part.astype(BF)
    kp[...] = nt(x[...], x[...])
    pl.semaphore_wait(barrier, len(peers))
    c_a = scatter_x(me, fl, send_a, slots_a, sems_a)
    c_k = []
    for k in (1, 2, 3):
        c_k.append(fl.start(kp, kr.at[k - 1], sems_k.at[0, k - 1], sems_k.at[1, k - 1], me.at_x(k)))

    landed(c_a)
    my_rows = rows_of(me.x, TQ)
    sums = []
    for i in range(4):
        total = acc_a[i, my_rows, :]
        for k in range(3):
            total = total + slots_a[k, i].astype(F32)
        sums.append(total)
    gate_pre, up_pre, gate_dot, up_dot = sums
    val, slope, curve = gelu_parts(gate_pre)
    slope_up = slope * up_pre
    hh[0, my_rows, :] = (val * up_pre).astype(BF)
    hh[1, my_rows, :] = (slope_up * gate_dot + val * up_dot).astype(BF)
    c_h = gather_x(me, fl, hh, sems_h)
    mm[0, my_rows, :] = slope_up
    mm[1, my_rows, :] = val
    c_m = gather_x(me, fl, mm, sems_m)
    own[0] = slope
    own[1] = up_pre * curve
    own[2] = gate_dot
    own[3] = up_dot
    landed(c_h)

    red = Reduce64(
        me, fl, 2, (red_b0, red_b1, red_b2, red_b3, red_b4, red_b5, red_b6, red_b7, red_b8, red_b9)
    )
    red.put(0, nt(hh[0], w_down[...]))
    red.put(1, nt(hh[1], w_down[...]) + nt(hh[0], s_down[...]))
    red.cores()
    red.ys()
    landed(c_k)
    total = kp[...] + (kr[0] + kr[1] + kr[2])
    high = total.astype(BF)
    kpair[0] = high
    kpair[1] = (total - high.astype(F32)).astype(BF)
    red.zs()

    def first_post(i, total, rows, lanes):
        if i == 0:
            total = total - target[rows, lanes].astype(F32)
        return (total / float(TOK)).astype(BF)

    red.finish(gg, first_post)

    part = nn(gg[0], w_down[...])
    acc_c[0] = part
    send_c[0] = part.astype(BF)
    part = nn(gg[1], w_down[...]) + nn(gg[0], s_down[...])
    acc_c[1] = part
    send_c[1] = part.astype(BF)
    c_c = scatter_x(me, fl, send_c, slots_c, sems_c)
    part = tn(gg[0], hh[1]) + tn(gg[1], hh[0])
    one[2] = part
    u1d[...] = part.astype(BF)
    landed(c_c)
    sums = []
    for i in range(2):
        total = acc_c[i, my_rows, :]
        for k in range(3):
            total = total + slots_c[k, i].astype(F32)
        sums.append(total)
    grad_hidden, back_dot = sums
    slope_term = grad_hidden * own[0]
    curve_term = grad_hidden * own[1]
    own[0] = slope_term
    own[1] = curve_term
    gu1[0, my_rows, :] = (
        back_dot * mm[0, my_rows, :] + slope_term * own[3] + curve_term * own[2]
    ).astype(BF)
    gu1[1, my_rows, :] = (back_dot * mm[1, my_rows, :] + slope_term * own[2]).astype(BF)
    c_g1 = gather_x(me, fl, gu1, sems_g1)
    landed(c_m)
    landed(c_g1)

    for i in range(2):
        tan2[i] = nn(kpair[0], gu1[i]) + nn(kpair[1], gu1[i])
    h2[...] = (mm[0] * tan2[0] + mm[1] * tan2[1]).astype(BF)
    red2 = Reduce64(
        me, fl, 1, (red_e0, red_e1, red_e2, red_e3, red_e4, red_e5, red_e6, red_e7, red_e8, red_e9)
    )
    red2.put(0, nt(h2[...], w_down[...]) + nt(hh[0], u1d[...]))
    red2.cores()
    red2.ys()
    for i in range(2):
        one[i] = nn(x_t[...], gu1[i])

    def dots_one(b, carry):
        rows = rows_of(b, BLK)
        ss, su, uu = carry
        for i in range(3):
            s = starts[i][rows, :].astype(F32) * SCALE
            u = one[i, rows, :] * SCALE
            ss = ss + fold(s * s)
            su = su + fold(s * u)
            uu = uu + fold(u * u)
        return ss, su, uu

    zero = jnp.zeros((8, HB), F32)
    ss, su, uu = lax.fori_loop(0, DB // BLK, dots_one, (zero, zero, zero))
    red2.zs()
    sum1 = ScalarSum(me, fl, sbuf1, ssem1)
    sum1.go(0, tile_of([whole_sum(ss), whole_sum(su), whole_sum(uu)]))
    sum1.go(1, sum1.get())
    red2.finish(g2, lambda i, total, rows, lanes: (total / float(TOK)).astype(BF))

    part = nn(g2[0], w_down[...]) + nn(gg[0], u1d[...])
    acc_f[0] = part
    send_f[0] = part.astype(BF)
    c_f = scatter_x(me, fl, send_f, slots_f, sems_f)
    sum1.go(2, sum1.get())
    two[2] = tn(gg[0], h2[...]) + tn(g2[0], hh[0])
    landed(c_f)
    back_dot = acc_f[0, my_rows, :]
    for k in range(3):
        back_dot = back_dot + slots_f[k, 0].astype(F32)
    gate_two = tan2[0, my_rows, :]
    up_two = tan2[1, my_rows, :]
    gu2[0, my_rows, :] = (
        back_dot * mm[0, my_rows, :] + own[0] * up_two + own[1] * gate_two
    ).astype(BF)
    gu2[1, my_rows, :] = (back_dot * mm[1, my_rows, :] + own[0] * gate_two).astype(BF)
    c_g2 = gather_x(me, fl, gu2, sems_g2)
    sum1.go(3, sum1.get())
    norms = sum1.get() * (1.0 / (SCALE * SCALE * ENTRIES))
    s_s, s_u, u_u = norms[0:1, 0:1], norms[1:2, 0:1], norms[2:3, 0:1]
    f = 1.0 / jnp.sqrt(s_s + EPS)
    v11 = f * f * s_s
    h11 = f * f * s_u
    w11 = f * f * u_u
    rr = jnp.maximum(w11 - h11 * h11 * (2.0 - v11), 0.0)
    h21 = jnp.sqrt(rr + EPS)
    v12 = (h11 - h11 * v11) / h21
    v22 = rr / (h21 * h21)
    a1 = f / h21
    a0 = -h11 * f / h21
    landed(c_g2)
    for i in range(2):
        two[i] = nn(x_t[...], gu2[i])

    def dots_two(b, carry):
        rows = rows_of(b, BLK)
        p1, p2, pw = carry
        for i in range(3):
            s = starts[i][rows, :].astype(F32)
            u = one[i, rows, :]
            w = (a1 * two[i, rows, :] + a0 * u) * SCALE
            first = f * s * SCALE
            second = (a1 * u + a0 * s) * SCALE
            p1 = p1 + fold(first * w)
            p2 = p2 + fold(second * w)
            pw = pw + fold(w * w)
        return p1, p2, pw

    p1, p2, pw = lax.fori_loop(0, DB // BLK, dots_two, (zero, zero, zero))
    sum2 = ScalarSum(me, fl, sbuf2, ssem2)
    tile = tile_of([whole_sum(p1), whole_sum(p2), whole_sum(pw)])
    for stage in range(4):
        sum2.go(stage, tile)
        tile = sum2.get()
    norms = tile * (1.0 / (SCALE * SCALE * ENTRIES))
    h12, h22, ww = norms[0:1, 0:1], norms[1:2, 0:1], norms[2:3, 0:1]
    rr = (
        ww
        - 2.0 * (h12 * h12 + h22 * h22)
        + h12 * h12 * v11
        + h22 * h22 * v22
        + 2.0 * h12 * h22 * v12
    )
    h32 = jnp.sqrt(jnp.maximum(rr, 0.0) + EPS)
    c2 = a1 / h32
    c1 = (a0 - h22 * a1) / h32
    c0 = -(h12 * f + h22 * a0) / h32
    scal[...] = tile_of([h21, h12, h22, h32, h11, c2, c1, c0])

    for copy in fl.sent:
        copy.wait_send()
    red.drain()
    red2.drain()


def rounds(*operands):
    dma = pltpu.SemaphoreType.DMA
    scratch = (
        [pltpu.VMEM((TOK, TOK), F32), pltpu.VMEM((3, TOK, TOK), F32), pltpu.VMEM((2, TOK, TOK), BF), dma((2, 3))]
        + [pltpu.VMEM((4, TOK, HB), F32), pltpu.VMEM((4, TOK, HB), BF), pltpu.VMEM((3, 4, TQ, HB), BF), dma((2, 3))]
        + [pltpu.VMEM((4, TQ, HB), F32), pltpu.VMEM((2, TOK, HB), BF), dma((2, 3)), pltpu.VMEM((2, TOK, HB), F32), dma((2, 3))]
        + reduce_scratch(2)
        + [pltpu.VMEM((2, TOK, DB), BF)]
        + [pltpu.VMEM((2, TOK, HB), F32), pltpu.VMEM((2, TOK, HB), BF), pltpu.VMEM((3, 2, TQ, HB), BF), dma((2, 3))]
        + [pltpu.VMEM((2, TOK, HB), BF), dma((2, 3)), pltpu.VMEM((DB, HB), BF), pltpu.VMEM((2, TOK, HB), F32), pltpu.VMEM((TOK, HB), BF)]
        + reduce_scratch(1)
        + [pltpu.VMEM((1, TOK, DB), BF)]
        + [pltpu.VMEM((1, TOK, HB), F32), pltpu.VMEM((1, TOK, HB), BF), pltpu.VMEM((3, 1, TQ, HB), BF), dma((2, 3))]
        + [pltpu.VMEM((2, TOK, HB), BF), dma((2, 3))]
        + [pltpu.VMEM((18, 8, 128), F32), dma((2, 18)), pltpu.VMEM((18, 8, 128), F32), dma((2, 18))]
    )
    return pl.pallas_call(
        kernel,
        out_shape=(
            jax.ShapeDtypeStruct((3, DB, HB), F32),
            jax.ShapeDtypeStruct((3, DB, HB), F32),
            jax.ShapeDtypeStruct((8, 128), F32),
        ),
        in_specs=[pl.BlockSpec(memory_space=pltpu.VMEM)] * 9,
        out_specs=[pl.BlockSpec(memory_space=pltpu.VMEM)] * 3,
        scratch_shapes=scratch,
        compiler_params=pltpu.CompilerParams(
            collective_id=0, has_side_effects=True, vmem_limit_bytes=58 * 1024 * 1024
        ),
        name="arnoldi",
    )(*operands)


def on_device(inputs, target, w_gate, w_up, w_down, start_gate, start_up, start_down):
    def regroup(w):
        return lax.all_to_all(w, "fsdp", split_axis=1, concat_axis=0, tiled=True)

    gate_cols, up_cols, start_gcols, start_ucols = map(regroup, (w_gate, w_up, start_gate, start_up))
    down_cols, start_dcols = map(regroup, (w_down.T, start_down.T))
    one, two, scal = rounds(
        inputs, inputs.T, target, gate_cols, up_cols, down_cols, start_gcols, start_ucols, start_dcols
    )
    c2, c1, c0 = scal[5, 0], scal[6, 0], scal[7, 0]
    third = [
        c2 * two[i] + c1 * one[i] + c0 * s.astype(F32)
        for i, s in enumerate((start_gcols, start_ucols, start_dcols))
    ]
    return (
        third[0].reshape(DB, 1, HB),
        third[1].reshape(DB, 1, HB),
        third[2].T.reshape(1, HB, DB),
        scal[0:4, 0],
        scal[4:5, 0],
    )


def solution(mesh):
    placed = (
        P(None, "dcn"),
        P(None, "dcn"),
        P(("dcn", "fsdp"), "tp"),
        P(("dcn", "fsdp"), "tp"),
        P("tp", ("dcn", "fsdp")),
        P(("dcn", "fsdp"), "tp"),
        P(("dcn", "fsdp"), "tp"),
        P("tp", ("dcn", "fsdp")),
    )
    return jax.shard_map(
        on_device,
        mesh=mesh,
        in_specs=placed,
        out_specs=(
            P("dcn", "tp", "fsdp"),
            P("dcn", "tp", "fsdp"),
            P("tp", "fsdp", "dcn"),
            P(),
            P(),
        ),
        check_vma=False,
    )
```

```python
import math

import jax
import jax.numpy as jnp
from jax import lax
from jax.experimental import pallas as pl
from jax.experimental.pallas import tpu as pltpu
from jax.sharding import PartitionSpec as P

D = 4608
FF = 18432
TOK = 320
DB = 1152
HB = 288
TQ = 80
RQ = 16
NRED = 5
LO = 640
LS = 512
BLK = 144
NF = 16
WR = 72
WL = 256
ENTRIES = float(3 * D * FF)
EPS = 1e-06
SCALE = 2.0**-14
MESH = pl.DeviceIdType.MESH
BF = jnp.bfloat16
F32 = jnp.float32

gelu_cubic = 0.044715
gelu_scale = math.sqrt(2.0 / math.pi)


def gelu_parts(argument):
    squared = argument * argument
    inner_arg = gelu_scale * (argument + gelu_cubic * squared * argument)
    tanh_val = jnp.tanh(inner_arg)
    sech_square = 1.0 - tanh_val * tanh_val
    inner_slope = gelu_scale * (1.0 + 3.0 * gelu_cubic * squared)
    inner_curve = gelu_scale * 6.0 * gelu_cubic * argument
    gelu_val = 0.5 * argument * (1.0 + tanh_val)
    gelu_slope = 0.5 * (1.0 + tanh_val) + 0.5 * argument * sech_square * inner_slope
    gelu_curve = sech_square * inner_slope + 0.5 * argument * (
        sech_square * inner_curve - 2.0 * tanh_val * sech_square * inner_slope * inner_slope
    )
    return (gelu_val, gelu_slope, gelu_curve)


def nn(a, b):
    return lax.dot_general(a, b, (((1,), (0,)), ((), ())), preferred_element_type=F32)


def nt(a, b):
    return lax.dot_general(a, b, (((1,), (1,)), ((), ())), preferred_element_type=F32)


def tn(a, b):
    return lax.dot_general(a, b, (((0,), (0,)), ((), ())), preferred_element_type=F32)


class Place:
    def __init__(self):
        self.x = lax.axis_index("dcn")
        fsdp = lax.axis_index("fsdp")
        tp = lax.axis_index("tp")
        self.f = fsdp
        self.t = tp
        self.y = fsdp // 4
        self.z = (tp // 2) * 4 + fsdp % 4
        self.c = tp % 2

    def dev(self, x=None, y=None, z=None, c=None):
        x = self.x if x is None else x
        y = self.y if y is None else y
        z = self.z if z is None else z
        c = self.c if c is None else c
        return (x, y * 4 + z % 4, (z // 4) * 2 + c)

    def at_x(self, k):
        return self.dev(x=(self.x + k) % 4)

    def at_y(self, k):
        return self.dev(y=(self.y + k) % 4)

    def at_z(self, k):
        return self.dev(z=(self.z + k) % 8)

    def at_f(self, k):
        return (self.x, (self.f + k) % NF, self.t)

    def across(self, low):
        return self.dev(z=(1 - self.z // 4) * 4 + low)

    def other(self):
        return self.dev(c=1 - self.c)


def rows_of(index, size):
    return pl.ds(pl.multiple_of(index * size, size), size)


def lanes_of(index, step, size):
    return pl.ds(pl.multiple_of(index * step, 128), size)


def remote(src, dst, ssem, rsem, dev):
    return pltpu.make_async_remote_copy(
        src_ref=src, dst_ref=dst, send_sem=ssem, recv_sem=rsem, device_id=dev, device_id_type=MESH
    )


class Flight:
    def __init__(self):
        self.sent = []

    def start(self, src, dst, ssem, rsem, dev):
        copy = remote(src, dst, ssem, rsem, dev)
        copy.start()
        self.sent.append(copy)
        return copy


def pack_wide(first, second, wide):
    for j in range(NF):
        lanes = slice(j * HB, j * HB + WL)
        both = jnp.concatenate([first[:, lanes].astype(F32), second[:, lanes].astype(F32)], axis=0)
        wide[j] = both.astype(BF)


def pack_rest(pairs, rest):
    lane = lax.broadcasted_iota(jnp.int32, (2 * WR, 128), 1)
    for j in range(NF):
        start = j * HB + WL
        base = start - start % 128
        total = jnp.zeros((2 * WR, 128), F32)
        for p, (first, second) in enumerate(pairs):
            both = jnp.concatenate(
                [first[:, base : base + 128].astype(F32), second[:, base : base + 128].astype(F32)], axis=0
            )
            shift = (32 * p - start) % 128
            if shift:
                both = pltpu.roll(both, shift, axis=1)
            total = jnp.where((lane >= 32 * p) & (lane < 32 * p + 32), both, total)
        rest[j] = total.astype(BF)


def unpack(p, wide, rest, first, second):
    for i in range(NF // 2):
        rows = slice(i * 2 * WR, (i + 1) * 2 * WR)
        a, b = wide[2 * i].astype(F32), wide[2 * i + 1].astype(F32)
        first[rows, 0:WL] = jnp.concatenate([a[:WR], b[:WR]], axis=0).astype(BF)
        second[rows, 0:WL] = jnp.concatenate([a[WR:], b[WR:]], axis=0).astype(BF)
        a, b = rest[2 * i].astype(F32), rest[2 * i + 1].astype(F32)
        if p:
            a, b = pltpu.roll(a, 128 - 32 * p, axis=1), pltpu.roll(b, 128 - 32 * p, axis=1)
        first[rows, WL:HB] = jnp.concatenate([a[:WR], b[:WR]], axis=0)[:, 0:32].astype(BF)
        second[rows, WL:HB] = jnp.concatenate([a[WR:], b[WR:]], axis=0)[:, 0:32].astype(BF)


def send_blocks(me, fl, out, land, ssems, rsems, lsem):
    copies = []
    for k in range(1, NF):
        copies.append(
            fl.start(out.at[(me.f + k) % NF], land.at[me.f], ssems.at[k], rsems.at[k], me.at_f(k))
        )
    own = pltpu.make_async_copy(out.at[me.f], land.at[me.f], lsem)
    own.start()
    return copies, own


def blocks_landed(flight):
    landed(flight[0])
    flight[1].wait()


def scatter_x(me, fl, stage, slots, sems):
    out = []
    for k in (1, 2, 3):
        peer = (me.x + k) % 4
        out.append(
            fl.start(
                stage.at[:, rows_of(peer, TQ), :],
                slots.at[k - 1],
                sems.at[0, k - 1],
                sems.at[1, k - 1],
                me.at_x(k),
            )
        )
    return out


def gather_x(me, fl, buf, sems):
    out = []
    mine = buf.at[:, rows_of(me.x, TQ), :]
    for k in (1, 2, 3):
        out.append(fl.start(mine, mine, sems.at[0, k - 1], sems.at[1, k - 1], me.at_x(k)))
    return out


def landed(copies):
    for copy in copies:
        copy.wait_recv()


class Reduce64:
    def __init__(self, me, fl, n, s):
        self.me, self.fl, self.n = me, fl, n
        (self.acc, self.send, self.r1, self.t1b, self.r2, self.t2b, self.r3, self.sems) = s

    def put(self, index, value):
        self.acc[index] = value
        self.send[index] = value.astype(BF)

    def cores(self):
        me = self.me
        self.c1 = self.fl.start(
            self.send.at[:, :, lanes_of(1 - me.c, LS, LO)],
            self.r1,
            self.sems.at[0, 0],
            self.sems.at[1, 0],
            me.other(),
        )

    def ys(self):
        me = self.me
        self.c1.wait_recv()
        for i in range(self.n):
            total = self.acc[i, :, lanes_of(me.c, LS, LO)] + self.r1[i].astype(F32)
            self.t1b[i] = total.astype(BF)
        self.c2 = []
        for k in (1, 2, 3):
            peer = (me.y + k) % 4
            self.c2.append(
                self.fl.start(
                    self.t1b.at[:, rows_of(peer, TQ), :],
                    self.r2.at[k - 1],
                    self.sems.at[0, k],
                    self.sems.at[1, k],
                    me.at_y(k),
                )
            )

    def zs(self):
        me = self.me
        landed(self.c2)
        for i in range(self.n):
            rows = rows_of(me.y, TQ)
            total = self.acc[i, rows, lanes_of(me.c, LS, LO)] + self.r1[i, rows, :].astype(F32)
            for k in range(3):
                total = total + self.r2[k, i].astype(F32)
            self.t2b[i] = total.astype(BF)
        for q in range(NRED):

            @pl.when(me.z != q)
            def _():
                remote(
                    self.t2b.at[:, q * RQ : (q + 1) * RQ, :],
                    self.r3.at[me.z],
                    self.sems.at[0, 4 + q],
                    self.sems.at[1, 4 + me.z],
                    me.dev(z=q),
                ).start()

    def finish(self, final, post):
        me = self.me
        mine = lanes_of(me.c, LS, LO)

        @pl.when(me.z < NRED)
        def _():
            self.r3[me.z] = self.t2b[:, rows_of(me.z, RQ), :]
            for s in range(8):

                @pl.when(me.z != s)
                def _():
                    remote(
                        self.t2b.at[:, 0:RQ, :],
                        self.r3.at[s],
                        self.sems.at[0, 4],
                        self.sems.at[1, 4 + s],
                        me.other(),
                    ).wait_recv()

            rows = pl.ds(pl.multiple_of(me.y * TQ + me.z * RQ, RQ), RQ)
            for i in range(self.n):
                total = self.r3[0, i].astype(F32)
                for s in range(1, 8):
                    total = total + self.r3[s, i].astype(F32)
                final[i, rows, mine] = post(i, total, rows, mine)
            for k in range(1, 8):
                piece = final.at[:, rows, mine]
                remote(piece, piece, self.sems.at[0, 11 + k], self.sems.at[1, 12 + me.z], me.at_z(k)).start()

        for q in range(NRED):
            piece = final.at[:, pl.ds(pl.multiple_of(me.y * TQ + q * RQ, RQ), RQ), mine]

            @pl.when(me.z != q)
            def _():
                remote(piece, piece, self.sems.at[0, 4], self.sems.at[1, 12 + q], me.other()).wait_recv()

        block = final.at[:, rows_of(me.y, TQ), mine]
        c5 = []
        for k in (1, 2, 3):
            c5.append(
                self.fl.start(block, block, self.sems.at[0, 19 + k], self.sems.at[1, 19 + k], me.at_y(k))
            )
        landed(c5)
        half = final.at[:, :, lanes_of(me.c, LO, LS)]
        c6 = self.fl.start(half, half, self.sems.at[0, 23], self.sems.at[1, 23], me.other())
        c6.wait_recv()

    def drain(self):
        me = self.me
        for q in range(NRED):

            @pl.when(me.z != q)
            def _():
                remote(
                    self.t2b.at[:, q * RQ : (q + 1) * RQ, :],
                    self.r3.at[me.z],
                    self.sems.at[0, 4 + q],
                    self.sems.at[1, 4 + me.z],
                    me.dev(z=q),
                ).wait_send()

        @pl.when(me.z < NRED)
        def _():
            for k in range(1, 8):
                remote(
                    self.t2b.at[:, 0:RQ, :],
                    self.t2b.at[:, 0:RQ, :],
                    self.sems.at[0, 11 + k],
                    self.sems.at[1, 12],
                    me.other(),
                ).wait_send()


def reduce_scratch(n):
    return [
        pltpu.VMEM((n, TOK, DB), F32),
        pltpu.VMEM((n, TOK, DB), BF),
        pltpu.VMEM((n, TOK, LO), BF),
        pltpu.VMEM((n, TOK, LO), BF),
        pltpu.VMEM((3, n, TQ, LO), BF),
        pltpu.VMEM((n, TQ, LO), BF),
        pltpu.VMEM((8, n, RQ, LO), BF),
        pltpu.SemaphoreType.DMA((2, 24)),
    ]


class ScalarSum:
    def __init__(self, me, fl, buf, sems):
        self.me, self.fl, self.buf, self.sems = me, fl, buf, sems

    def go(self, stage, tile):
        me = self.me
        count, index, base, at = (
            (2, me.c, 0, lambda k: me.other()),
            (4, me.x, 2, me.at_x),
            (4, me.y, 6, me.at_y),
            (8, me.z, 10, me.at_z),
        )[stage]
        mine = self.buf.at[base + index]
        self.buf[base + index] = tile
        self.copies = []
        for k in range(1, count):
            self.copies.append(
                self.fl.start(mine, mine, self.sems.at[0, base + k], self.sems.at[1, base + k], at(k))
            )
        self.span = (base, count)

    def get(self):
        landed(self.copies)
        base, count = self.span
        total = self.buf[base]
        for s in range(1, count):
            total = total + self.buf[base + s]
        return total


def rsqrt_of(value):
    return 1.0 / jnp.sqrt(value)


def whole_sum(value):
    return jnp.sum(jnp.sum(value, axis=1, keepdims=True), axis=0, keepdims=True)


def fold(value):
    return jnp.sum(value.reshape(BLK // 8, 8, HB), axis=0)


def tile_of(values):
    rows = [jnp.broadcast_to(v, (1, 128)) for v in values]
    while len(rows) < 8:
        rows.append(jnp.zeros((1, 128), F32))
    return jnp.concatenate(rows, axis=0)


def kernel(
    x, x_t, target, in_wg, in_wu, in_wd, in_sg, in_su, in_sd,
    out_g, out_u, out_d, scal,
    wide_s, wide_r, rest_s, rest_r, sems_w, sems_l,
    w_gate, w_up, w_down, s_gate, s_up, s_down, one, two,
    kp, kr, kpair, sems_k,
    acc_a, send_a, slots_a, sems_a,
    own, hh, sems_h, mm, sems_m,
    red_b0, red_b1, red_b2, red_b3, red_b4, red_b5, red_b6, red_b7,
    gg,
    acc_c, send_c, slots_c, sems_c,
    gu1, sems_g1, u1d, tan2, h2,
    red_e0, red_e1, red_e2, red_e3, red_e4, red_e5, red_e6, red_e7,
    g2,
    acc_f, send_f, slots_f, sems_f,
    gu2, sems_g2,
    sbuf1, ssem1, sbuf2, ssem2,
):
    me = Place()
    fl = Flight()
    starts = (s_gate, s_up, s_down)
    twos = (out_g, out_u, two)

    barrier = pltpu.get_barrier_semaphore()
    peers = (
        [me.at_f(k) for k in range(1, NF)]
        + [me.at_x(k) for k in (1, 2, 3)]
        + [me.across(low) for low in range(4)]
        + [me.other()]
    )
    for peer in peers:
        pl.semaphore_signal(barrier, inc=1, device_id=peer, device_id_type=MESH)

    pairs = ((in_wg, in_wu), (in_sg, in_su), (in_wd, in_sd))
    flights = []
    with jax.named_scope("pack"):
        pack_wide(*pairs[0], wide_s.at[0])
    with jax.named_scope("entry"):
        pl.semaphore_wait(barrier, len(peers))
    with jax.named_scope("send_blocks"):
        flights.append(
            send_blocks(me, fl, wide_s.at[0], wide_r.at[0], sems_w.at[0, 0], sems_w.at[1, 0], sems_l.at[0])
        )
        pack_rest(pairs, rest_s)
        flights.append(send_blocks(me, fl, rest_s, rest_r, sems_w.at[0, 3], sems_w.at[1, 3], sems_l.at[3]))
        for p in (1, 2):
            pack_wide(*pairs[p], wide_s.at[p])
            flights.append(
                send_blocks(
                    me, fl, wide_s.at[p], wide_r.at[p], sems_w.at[0, p], sems_w.at[1, p], sems_l.at[p]
                )
            )
    with jax.named_scope("gram"):
        kp[...] = nt(x[...], x[...])
        c_k = []
        for k in (1, 2, 3):
            c_k.append(fl.start(kp, kr.at[k - 1], sems_k.at[0, k - 1], sems_k.at[1, k - 1], me.at_x(k)))

    def forward(base, first, second):
        for i, w in enumerate((first, second)):
            part = nn(x[...], w[...])
            acc_a[base + i] = part
            send_a[base + i] = part.astype(BF)

    with jax.named_scope("wait_w"):
        blocks_landed(flights[0])
        blocks_landed(flights[1])
    with jax.named_scope("unpack_w"):
        unpack(0, wide_r.at[0], rest_r, w_gate, w_up)
        forward(0, w_gate, w_up)
    with jax.named_scope("wait_s"):
        blocks_landed(flights[2])
    with jax.named_scope("unpack_s"):
        unpack(1, wide_r.at[1], rest_r, s_gate, s_up)
        forward(2, s_gate, s_up)
    c_a = scatter_x(me, fl, send_a, slots_a, sems_a)

    with jax.named_scope("wait_a"):
        landed(c_a)
    my_rows = rows_of(me.x, TQ)
    sums = []
    for i in range(4):
        total = acc_a[i, my_rows, :]
        for k in range(3):
            total = total + slots_a[k, i].astype(F32)
        sums.append(total)
    gate_pre, up_pre, gate_dot, up_dot = sums
    val, slope, curve = gelu_parts(gate_pre)
    slope_up = slope * up_pre
    hh[0, my_rows, :] = (val * up_pre).astype(BF)
    hh[1, my_rows, :] = (slope_up * gate_dot + val * up_dot).astype(BF)
    c_h = gather_x(me, fl, hh, sems_h)
    mm[0, my_rows, :] = slope_up
    mm[1, my_rows, :] = val
    c_m = gather_x(me, fl, mm, sems_m)
    own[0] = slope
    own[1] = up_pre * curve
    own[2] = gate_dot
    own[3] = up_dot
    with jax.named_scope("wait_h"):
        landed(c_h)
    with jax.named_scope("wait_d"):
        blocks_landed(flights[3])
    with jax.named_scope("unpack_d"):
        unpack(2, wide_r.at[2], rest_r, w_down, s_down)

    red = Reduce64(
        me, fl, 2, (red_b0, red_b1, red_b2, red_b3, red_b4, red_b5, red_b6, red_b7)
    )
    with jax.named_scope("out"):
        red.put(0, nt(hh[0], w_down[...]))
        red.put(1, nt(hh[1], w_down[...]) + nt(hh[0], s_down[...]))
    red.cores()
    with jax.named_scope("core_sum"):
        red.ys()
    landed(c_k)
    total = kp[...] + (kr[0] + kr[1] + kr[2])
    high = total.astype(BF)
    kpair[0] = high
    kpair[1] = (total - high.astype(F32)).astype(BF)
    with jax.named_scope("y_sum"):
        red.zs()

    def first_post(i, total, rows, lanes):
        if i == 0:
            total = total - target[rows, lanes].astype(F32)
        return (total / float(TOK)).astype(BF)

    with jax.named_scope("z_sum"):
        red.finish(gg, first_post)

    with jax.named_scope("back"):
        part = nn(gg[0], w_down[...])
        acc_c[0] = part
        send_c[0] = part.astype(BF)
        part = nn(gg[1], w_down[...]) + nn(gg[0], s_down[...])
        acc_c[1] = part
        send_c[1] = part.astype(BF)
    c_c = scatter_x(me, fl, send_c, slots_c, sems_c)
    with jax.named_scope("u1d"):
        part = tn(gg[0], hh[1]) + tn(gg[1], hh[0])
        one[2] = part
        u1d[...] = part.astype(BF)
    with jax.named_scope("wait_c"):
        landed(c_c)
    sums = []
    for i in range(2):
        total = acc_c[i, my_rows, :]
        for k in range(3):
            total = total + slots_c[k, i].astype(F32)
        sums.append(total)
    grad_hidden, back_dot = sums
    slope_term = grad_hidden * own[0]
    curve_term = grad_hidden * own[1]
    own[0] = slope_term
    own[1] = curve_term
    gu1[0, my_rows, :] = (
        back_dot * mm[0, my_rows, :] + slope_term * own[3] + curve_term * own[2]
    ).astype(BF)
    gu1[1, my_rows, :] = (back_dot * mm[1, my_rows, :] + slope_term * own[2]).astype(BF)
    c_g1 = gather_x(me, fl, gu1, sems_g1)
    with jax.named_scope("wait_g1"):
        landed(c_m)
        landed(c_g1)

    with jax.named_scope("second"):
        for i in range(2):
            tan2[i] = nn(kpair[0], gu1[i]) + nn(kpair[1], gu1[i])
        h2[...] = (mm[0] * tan2[0] + mm[1] * tan2[1]).astype(BF)
    red2 = Reduce64(
        me, fl, 1, (red_e0, red_e1, red_e2, red_e3, red_e4, red_e5, red_e6, red_e7)
    )
    with jax.named_scope("out2"):
        red2.put(0, nt(h2[...], w_down[...]) + nt(hh[0], u1d[...]))
    red2.cores()
    with jax.named_scope("core_sum2"):
        red2.ys()
    with jax.named_scope("image"):
        for i in range(2):
            one[i] = nn(x_t[...], gu1[i])

    def dots_one(b, carry):
        rows = rows_of(b, BLK)
        ss, su, uu = carry
        for i in range(3):
            s = starts[i][rows, :].astype(F32) * SCALE
            u = one[i, rows, :] * SCALE
            ss = ss + fold(s * s)
            su = su + fold(s * u)
            uu = uu + fold(u * u)
        return ss, su, uu

    zero = jnp.zeros((8, HB), F32)
    with jax.named_scope("dots"):
        ss, su, uu = lax.fori_loop(0, DB // BLK, dots_one, (zero, zero, zero))
    with jax.named_scope("y_sum2"):
        red2.zs()
    sum1 = ScalarSum(me, fl, sbuf1, ssem1)
    with jax.named_scope("scal"):
        sum1.go(0, tile_of([whole_sum(ss), whole_sum(su), whole_sum(uu)]))
        sum1.go(1, sum1.get())
    with jax.named_scope("z_sum2"):
        red2.finish(g2, lambda i, total, rows, lanes: (total / float(TOK)).astype(BF))

    with jax.named_scope("back2"):
        part = nn(g2[0], w_down[...]) + nn(gg[0], u1d[...])
        acc_f[0] = part
        send_f[0] = part.astype(BF)
    c_f = scatter_x(me, fl, send_f, slots_f, sems_f)
    with jax.named_scope("u2d"):
        sum1.go(2, sum1.get())
        two[...] = tn(gg[0], h2[...]) + tn(g2[0], hh[0])
    with jax.named_scope("wait_f"):
        landed(c_f)
    back_dot = acc_f[0, my_rows, :]
    for k in range(3):
        back_dot = back_dot + slots_f[k, 0].astype(F32)
    gate_two = tan2[0, my_rows, :]
    up_two = tan2[1, my_rows, :]
    gu2[0, my_rows, :] = (
        back_dot * mm[0, my_rows, :] + own[0] * up_two + own[1] * gate_two
    ).astype(BF)
    gu2[1, my_rows, :] = (back_dot * mm[1, my_rows, :] + own[0] * gate_two).astype(BF)
    c_g2 = gather_x(me, fl, gu2, sems_g2)
    with jax.named_scope("scal2"):
        sum1.go(3, sum1.get())
    norms = sum1.get() * (1.0 / (SCALE * SCALE * ENTRIES))
    s_s, s_u, u_u = norms[0:1, 0:1], norms[1:2, 0:1], norms[2:3, 0:1]
    f = 1.0 / jnp.sqrt(s_s + EPS)
    v11 = f * f * s_s
    h11 = f * f * s_u
    w11 = f * f * u_u
    rr = jnp.maximum(w11 - h11 * h11 * (2.0 - v11), 0.0)
    h21 = jnp.sqrt(rr + EPS)
    v12 = (h11 - h11 * v11) / h21
    v22 = rr / (h21 * h21)
    a1 = f / h21
    a0 = -h11 * f / h21
    with jax.named_scope("wait_g2"):
        landed(c_g2)
    with jax.named_scope("image2"):
        for i in range(2):
            twos[i][...] = nn(x_t[...], gu2[i])

    def dots_two(b, carry):
        rows = rows_of(b, BLK)
        p1, p2, pw = carry
        for i in range(3):
            s = starts[i][rows, :].astype(F32)
            u = one[i, rows, :]
            w = (a1 * twos[i][rows, :] + a0 * u) * SCALE
            first = f * s * SCALE
            second = (a1 * u + a0 * s) * SCALE
            p1 = p1 + fold(first * w)
            p2 = p2 + fold(second * w)
            pw = pw + fold(w * w)
        return p1, p2, pw

    with jax.named_scope("dots2"):
        p1, p2, pw = lax.fori_loop(0, DB // BLK, dots_two, (zero, zero, zero))
    sum2 = ScalarSum(me, fl, sbuf2, ssem2)
    tile = tile_of([whole_sum(p1), whole_sum(p2), whole_sum(pw)])
    with jax.named_scope("scal3"):
        for stage in range(4):
            sum2.go(stage, tile)
            tile = sum2.get()
    norms = tile * (1.0 / (SCALE * SCALE * ENTRIES))
    h12, h22, ww = norms[0:1, 0:1], norms[1:2, 0:1], norms[2:3, 0:1]
    rr = (
        ww
        - 2.0 * (h12 * h12 + h22 * h22)
        + h12 * h12 * v11
        + h22 * h22 * v22
        + 2.0 * h12 * h22 * v12
    )
    h32 = jnp.sqrt(jnp.maximum(rr, 0.0) + EPS)
    c2 = a1 / h32
    c1 = (a0 - h22 * a1) / h32
    c0 = -(h12 * f + h22 * a0) / h32
    scal[...] = tile_of([h21, h12, h22, h32, h11])
    with jax.named_scope("third"):
        for i, out in enumerate((out_g, out_u)):
            def third(b, carry, i=i, out=out):
                rows = rows_of(b, BLK)
                out[rows, :] = c2 * twos[i][rows, :] + c1 * one[i, rows, :] + c0 * starts[i][rows, :].astype(F32)
                return carry

            lax.fori_loop(0, DB // BLK, third, 0)
        for b in range(DB // 128):
            rows = slice(b * 128, (b + 1) * 128)
            value = c2 * two[rows, :] + c1 * one[2, rows, :] + c0 * s_down[rows, :].astype(F32)
            out_d[:, rows] = value.T

    for copy in fl.sent:
        copy.wait_send()
    red.drain()
    red2.drain()


def rounds(*operands):
    dma = pltpu.SemaphoreType.DMA
    scratch = (
        [pltpu.VMEM((3, NF, 2 * WR, WL), BF)] * 2
        + [pltpu.VMEM((NF, 2 * WR, 128), BF)] * 2
        + [dma((2, 4, NF)), dma((4,))]
        + [pltpu.VMEM((DB, HB), BF)] * 6
        + [pltpu.VMEM((3, DB, HB), F32), pltpu.VMEM((DB, HB), F32)]
        + [pltpu.VMEM((TOK, TOK), F32), pltpu.VMEM((3, TOK, TOK), F32), pltpu.VMEM((2, TOK, TOK), BF), dma((2, 3))]
        + [pltpu.VMEM((4, TOK, HB), F32), pltpu.VMEM((4, TOK, HB), BF), pltpu.VMEM((3, 4, TQ, HB), BF), dma((2, 3))]
        + [pltpu.VMEM((4, TQ, HB), F32), pltpu.VMEM((2, TOK, HB), BF), dma((2, 3)), pltpu.VMEM((2, TOK, HB), F32), dma((2, 3))]
        + reduce_scratch(2)
        + [pltpu.VMEM((2, TOK, DB), BF)]
        + [pltpu.VMEM((2, TOK, HB), F32), pltpu.VMEM((2, TOK, HB), BF), pltpu.VMEM((3, 2, TQ, HB), BF), dma((2, 3))]
        + [pltpu.VMEM((2, TOK, HB), BF), dma((2, 3)), pltpu.VMEM((DB, HB), BF), pltpu.VMEM((2, TOK, HB), F32), pltpu.VMEM((TOK, HB), BF)]
        + reduce_scratch(1)
        + [pltpu.VMEM((1, TOK, DB), BF)]
        + [pltpu.VMEM((1, TOK, HB), F32), pltpu.VMEM((1, TOK, HB), BF), pltpu.VMEM((3, 1, TQ, HB), BF), dma((2, 3))]
        + [pltpu.VMEM((2, TOK, HB), BF), dma((2, 3))]
        + [pltpu.VMEM((18, 8, 128), F32), dma((2, 18)), pltpu.VMEM((18, 8, 128), F32), dma((2, 18))]
    )
    return pl.pallas_call(
        kernel,
        out_shape=(
            jax.ShapeDtypeStruct((DB, HB), F32),
            jax.ShapeDtypeStruct((DB, HB), F32),
            jax.ShapeDtypeStruct((HB, DB), F32),
            jax.ShapeDtypeStruct((8, 128), F32),
        ),
        in_specs=[pl.BlockSpec(memory_space=pltpu.VMEM)] * 9,
        out_specs=[pl.BlockSpec(memory_space=pltpu.VMEM)] * 4,
        scratch_shapes=scratch,
        compiler_params=pltpu.CompilerParams(
            collective_id=0, has_side_effects=True, vmem_limit_bytes=60 * 1024 * 1024
        ),
        name="arnoldi",
    )(*operands)


def on_device(inputs, target, w_gate, w_up, w_down, start_gate, start_up, start_down):
    third_g, third_u, third_d, scal = rounds(
        inputs, inputs.T, target, w_gate, w_up, w_down.T, start_gate, start_up, start_down.T
    )
    return (
        third_g.reshape(DB, 1, HB),
        third_u.reshape(DB, 1, HB),
        third_d.reshape(1, HB, DB),
        scal[0:4, 0],
        scal[4:5, 0],
    )


def solution(mesh):
    placed = (
        P(None, "dcn"),
        P(None, "dcn"),
        P(("dcn", "fsdp"), "tp"),
        P(("dcn", "fsdp"), "tp"),
        P("tp", ("dcn", "fsdp")),
        P(("dcn", "fsdp"), "tp"),
        P(("dcn", "fsdp"), "tp"),
        P("tp", ("dcn", "fsdp")),
    )
    return jax.shard_map(
        on_device,
        mesh=mesh,
        in_specs=placed,
        out_specs=(
            P("dcn", "tp", "fsdp"),
            P("dcn", "tp", "fsdp"),
            P("tp", "fsdp", "dcn"),
            P(),
            P(),
        ),
        check_vma=False,
    )
```

```python
import math

import jax
import jax.numpy as jnp
from jax import lax
from jax.experimental import pallas as pl
from jax.experimental.pallas import tpu as pltpu
from jax.sharding import PartitionSpec as P

D = 4608
FF = 18432
TOK = 320
DB = 1152
HB = 288
TQ = 80
RQ = 16
NRED = 5
BLK = 48
NF = 16
WR = 72
WL = 256
ENTRIES = float(3 * D * FF)
EPS = 1e-06
SCALE = 2.0**-14
MESH = pl.DeviceIdType.MESH
BF = jnp.bfloat16
F32 = jnp.float32

gelu_cubic = 0.044715
gelu_scale = math.sqrt(2.0 / math.pi)


def gelu_parts(argument):
    squared = argument * argument
    inner_arg = gelu_scale * (argument + gelu_cubic * squared * argument)
    tanh_val = jnp.tanh(inner_arg)
    sech_square = 1.0 - tanh_val * tanh_val
    inner_slope = gelu_scale * (1.0 + 3.0 * gelu_cubic * squared)
    inner_curve = gelu_scale * 6.0 * gelu_cubic * argument
    gelu_val = 0.5 * argument * (1.0 + tanh_val)
    gelu_slope = 0.5 * (1.0 + tanh_val) + 0.5 * argument * sech_square * inner_slope
    gelu_curve = sech_square * inner_slope + 0.5 * argument * (
        sech_square * inner_curve - 2.0 * tanh_val * sech_square * inner_slope * inner_slope
    )
    return (gelu_val, gelu_slope, gelu_curve)


def nn(a, b):
    return lax.dot_general(a, b, (((1,), (0,)), ((), ())), preferred_element_type=F32)


def nt(a, b):
    return lax.dot_general(a, b, (((1,), (1,)), ((), ())), preferred_element_type=F32)


def tn(a, b):
    return lax.dot_general(a, b, (((0,), (0,)), ((), ())), preferred_element_type=F32)


class Place:
    def __init__(self):
        self.x = lax.axis_index("dcn")
        fsdp = lax.axis_index("fsdp")
        tp = lax.axis_index("tp")
        self.f = fsdp
        self.t = tp
        self.y = fsdp // 4
        self.z = (tp // 2) * 4 + fsdp % 4
        self.c = tp % 2

    def dev(self, x=None, y=None, z=None, c=None):
        x = self.x if x is None else x
        y = self.y if y is None else y
        z = self.z if z is None else z
        c = self.c if c is None else c
        return (x, y * 4 + z % 4, (z // 4) * 2 + c)

    def at_x(self, k):
        return self.dev(x=(self.x + k) % 4)

    def at_y(self, k):
        return self.dev(y=(self.y + k) % 4)

    def at_z(self, k):
        return self.dev(z=(self.z + k) % 8)

    def at_f(self, k):
        return (self.x, (self.f + k) % NF, self.t)

    def at_t(self, k):
        return (self.x, self.f, (self.t + k) % 4)

    def across(self, low):
        return self.dev(z=(1 - self.z // 4) * 4 + low)

    def other(self):
        return self.dev(c=1 - self.c)


def rows_of(index, size):
    return pl.ds(pl.multiple_of(index * size, size), size)


def lanes_at(start, size):
    return pl.ds(pl.multiple_of(start, 128), size)


def remote(src, dst, ssem, rsem, dev):
    return pltpu.make_async_remote_copy(
        src_ref=src, dst_ref=dst, send_sem=ssem, recv_sem=rsem, device_id=dev, device_id_type=MESH
    )


class Flight:
    def __init__(self):
        self.sent = []

    def start(self, src, dst, ssem, rsem, dev):
        copy = remote(src, dst, ssem, rsem, dev)
        copy.start()
        self.sent.append(copy)
        return copy


def pack_wide(first, second, wide):
    for j in range(NF):
        lanes = slice(j * HB, j * HB + WL)
        both = jnp.concatenate([first[:, lanes].astype(F32), second[:, lanes].astype(F32)], axis=0)
        wide[j] = both.astype(BF)


def pack_rest(pairs, rest):
    lane = lax.broadcasted_iota(jnp.int32, (2 * WR, 128), 1)
    for j in range(NF):
        start = j * HB + WL
        base = start - start % 128
        total = jnp.zeros((2 * WR, 128), F32)
        for p, (first, second) in enumerate(pairs):
            both = jnp.concatenate(
                [first[:, base : base + 128].astype(F32), second[:, base : base + 128].astype(F32)], axis=0
            )
            shift = (32 * p - start) % 128
            if shift:
                both = pltpu.roll(both, shift, axis=1)
            total = jnp.where((lane >= 32 * p) & (lane < 32 * p + 32), both, total)
        rest[j] = total.astype(BF)


def unpack(p, wide, rest, first, second):
    for i in range(NF // 2):
        rows = slice(i * 2 * WR, (i + 1) * 2 * WR)
        a, b = wide[2 * i].astype(F32), wide[2 * i + 1].astype(F32)
        first[rows, 0:WL] = jnp.concatenate([a[:WR], b[:WR]], axis=0).astype(BF)
        second[rows, 0:WL] = jnp.concatenate([a[WR:], b[WR:]], axis=0).astype(BF)
        a, b = rest[2 * i].astype(F32), rest[2 * i + 1].astype(F32)
        if p:
            a, b = pltpu.roll(a, 128 - 32 * p, axis=1), pltpu.roll(b, 128 - 32 * p, axis=1)
        first[rows, WL:HB] = jnp.concatenate([a[:WR], b[:WR]], axis=0)[:, 0:32].astype(BF)
        second[rows, WL:HB] = jnp.concatenate([a[WR:], b[WR:]], axis=0)[:, 0:32].astype(BF)


def send_blocks(me, fl, out, land, ssems, rsems, lsem):
    copies = []
    for k in range(1, NF):
        copies.append(
            fl.start(out.at[(me.f + k) % NF], land.at[me.f], ssems.at[k], rsems.at[k], me.at_f(k))
        )
    own = pltpu.make_async_copy(out.at[me.f], land.at[me.f], lsem)
    own.start()
    return copies, own


def blocks_landed(flight):
    landed(flight[0])
    flight[1].wait()


def scatter_x(me, fl, stage, slots, sems):
    out = []
    for k in (1, 2, 3):
        peer = (me.x + k) % 4
        out.append(
            fl.start(
                stage.at[:, rows_of(peer, TQ), :],
                slots.at[k - 1],
                sems.at[0, k - 1],
                sems.at[1, k - 1],
                me.at_x(k),
            )
        )
    return out


def gather_x(me, fl, buf, sems):
    out = []
    mine = buf.at[:, rows_of(me.x, TQ), :]
    for k in (1, 2, 3):
        out.append(fl.start(mine, mine, sems.at[0, k - 1], sems.at[1, k - 1], me.at_x(k)))
    return out


def landed(copies):
    for copy in copies:
        copy.wait_recv()


class Chunk:
    def __init__(self, me, fl, acc, send, scratch, low, width, back, back_width):
        self.me, self.fl, self.acc, self.send = me, fl, acc, send
        (self.r1, self.t1b, self.r2, self.t2b, self.r3, self.sems) = scratch
        self.mine = lanes_at(low(me.c), width)
        self.theirs = lanes_at(low(1 - me.c), width)
        self.back = lanes_at(back(me.c), back_width)

    def go(self, src, dst, sem, dev, rsem=None):
        return self.fl.start(src, dst, self.sems.at[0, sem], self.sems.at[1, sem], dev)

    def put(self, value):
        self.acc[...] = value
        self.send[...] = value.astype(BF)

    def cores(self):
        me = self.me
        self.c1 = {}
        for k in (1, 2, 3, 0):
            rows = rows_of((me.y + k) % 4, TQ)
            self.c1[k] = self.go(self.send.at[rows, self.theirs], self.r1.at[rows, :], k, me.other())

    def ys(self):
        me = self.me
        self.c2 = []
        for k in (1, 2, 3):
            landed([self.c1[k]])
            rows = rows_of((me.y + k) % 4, TQ)
            self.t1b[rows, :] = (self.acc[rows, self.mine] + self.r1[rows, :].astype(F32)).astype(BF)
            self.c2.append(self.go(self.t1b.at[rows, :], self.r2.at[k - 1], 3 + k, me.at_y(k)))

    def zs(self):
        me = self.me
        landed([self.c1[0]])
        rows = rows_of(me.y, TQ)
        total = self.acc[rows, self.mine] + self.r1[rows, :].astype(F32)
        landed(self.c2)
        for k in range(3):
            total = total + self.r2[k].astype(F32)
        self.t2b[...] = total.astype(BF)
        for q in range(NRED):

            @pl.when(me.z != q)
            def _():
                remote(
                    self.t2b.at[q * RQ : (q + 1) * RQ, :],
                    self.r3.at[me.z],
                    self.sems.at[0, 7 + q],
                    self.sems.at[1, 7 + me.z],
                    me.dev(z=q),
                ).start()

    def reduce(self, final, post):
        me = self.me
        self.final = final

        @pl.when(me.z < NRED)
        def _():
            self.r3[me.z] = self.t2b[rows_of(me.z, RQ), :]
            for s in range(8):

                @pl.when(me.z != s)
                def _():
                    remote(
                        self.t2b.at[0:RQ, :],
                        self.r3.at[s],
                        self.sems.at[0, 7],
                        self.sems.at[1, 7 + s],
                        me.other(),
                    ).wait_recv()

            rows = pl.ds(pl.multiple_of(me.y * TQ + me.z * RQ, RQ), RQ)
            total = self.r3[0].astype(F32)
            for s in range(1, 8):
                total = total + self.r3[s].astype(F32)
            final[rows, self.mine] = post(total, rows, self.mine)
            for k in range(1, 8):
                piece = final.at[rows, self.mine]
                remote(
                    piece, piece, self.sems.at[0, 14 + k], self.sems.at[1, 15 + me.z], me.at_z(k)
                ).start()

    def spread(self):
        me, final = self.me, self.final
        for q in range(NRED):
            piece = final.at[pl.ds(pl.multiple_of(me.y * TQ + q * RQ, RQ), RQ), self.mine]

            @pl.when(me.z != q)
            def _():
                remote(piece, piece, self.sems.at[0, 7], self.sems.at[1, 15 + q], me.other()).wait_recv()

        rows = rows_of(me.y, TQ)
        block = final.at[rows, self.mine]
        self.c5 = [self.go(block, block, 21 + k, me.at_y(k)) for k in (1, 2, 3)]
        block = final.at[rows, self.back]
        self.c6 = [self.go(block, block, 25, me.other())]

    def collect(self):
        me, final = self.me, self.final
        for k in (1, 2, 3):
            landed([self.c5[k - 1]])
            block = final.at[rows_of((me.y + 4 - k) % 4, TQ), self.back]
            self.c6.append(self.go(block, block, 25 + k, me.other()))
        landed(self.c6)

    def drain(self):
        me = self.me
        for q in range(NRED):

            @pl.when(me.z != q)
            def _():
                remote(
                    self.t2b.at[q * RQ : (q + 1) * RQ, :],
                    self.r3.at[me.z],
                    self.sems.at[0, 7 + q],
                    self.sems.at[1, 7 + me.z],
                    me.dev(z=q),
                ).wait_send()

        @pl.when(me.z < NRED)
        def _():
            for k in range(1, 8):
                remote(
                    self.t2b.at[0:RQ, :],
                    self.t2b.at[0:RQ, :],
                    self.sems.at[0, 14 + k],
                    self.sems.at[1, 15],
                    me.other(),
                ).wait_send()


def chunk_scratch(width):
    return [
        pltpu.VMEM((TOK, width), BF),
        pltpu.VMEM((TOK, width), BF),
        pltpu.VMEM((3, TQ, width), BF),
        pltpu.VMEM((TQ, width), BF),
        pltpu.VMEM((8, RQ, width), BF),
        pltpu.SemaphoreType.DMA((2, 30)),
    ]


class ScalarSum:
    def __init__(self, me, fl, buf, sems):
        self.me, self.fl, self.buf, self.sems = me, fl, buf, sems

    def go(self, stage, tile):
        me = self.me
        index, base, count, at = (
            (me.x, 0, 4, me.at_x),
            (me.f, 4, 16, me.at_f),
            (me.t, 20, 4, me.at_t),
        )[stage]
        mine = self.buf.at[base + index]
        self.buf[base + index] = tile
        self.copies = []
        for k in range(1, count):
            self.copies.append(
                self.fl.start(mine, mine, self.sems.at[0, base + k], self.sems.at[1, base + k], at(k))
            )
        self.span = (base, count)

    def get(self):
        landed(self.copies)
        base, count = self.span
        total = self.buf[base]
        for s in range(1, count):
            total = total + self.buf[base + s]
        return total


def whole_sum(value):
    return jnp.sum(jnp.sum(value, axis=1, keepdims=True), axis=0, keepdims=True)


def fold(value):
    return jnp.sum(value.reshape(BLK // 8, 8, DB), axis=0)


def tile_of(values):
    rows = [jnp.broadcast_to(v, (1, 128)) for v in values]
    while len(rows) < 8:
        rows.append(jnp.zeros((1, 128), F32))
    return jnp.concatenate(rows, axis=0)


def add_x(acc, slots, rows, i):
    total = acc[i, rows, :]
    for k in range(3):
        total = total + slots[k, i].astype(F32)
    return total


def whole_low(c):
    return c * 512


def whole_back(c):
    return c * 640


def outer_low(c):
    return c * 768


def inner_low(c):
    return 384 + c * 128


def inner_back(c):
    return 384 + c * 256


def kernel(
    x, target, in_wg, in_wu, in_wd, in_sg, in_su, in_sd,
    out_g, out_u, out_d, hess, ray,
    wide_s, wide_r, rest_s, rest_r, sems_w, sems_l,
    w_gate, w_up, w_down, s_gate, s_up, s_down, start_t, one,
    kp, kr, kpair, sems_k,
    acc_a, send_a, slots_a, sems_a, acc_d, send_d, slots_d, sems_d,
    own, hh, sems_h, mm, sems_m,
    acc_o, send_o, acc_p, send_p,
    o0, o1, o2, o3, o4, o5, p0, p1, p2, p3, p4, p5,
    go, gd,
    acc_b, send_b, slots_b, sems_b, acc_c, send_c, slots_c, sems_c,
    gu1, sems_g1, u1d, tan2, h2,
    q0, q1, q2, q3, q4, q5, r0, r1, r2, r3, r4, r5,
    g2,
    acc_f, send_f, slots_f, sems_f,
    gu2, sems_g2,
    sbuf1, ssem1, sbuf2, ssem2,
):
    me = Place()
    fl = Flight()
    twos = (out_g, out_u, out_d)

    barrier = pltpu.get_barrier_semaphore()
    peers = (
        [me.at_f(k) for k in range(1, NF)]
        + [me.at_t(k) for k in (1, 2, 3)]
        + [me.at_x(k) for k in (1, 2, 3)]
        + [me.across(low) for low in range(4)]
    )
    for peer in peers:
        pl.semaphore_signal(barrier, inc=1, device_id=peer, device_id_type=MESH)

    pairs = ((in_wg, in_wu), (in_sg, in_su), (in_wd, in_sd))
    flights = []

    def send_wide(p):
        flights.append(
            send_blocks(me, fl, wide_s.at[p], wide_r.at[p], sems_w.at[0, p], sems_w.at[1, p], sems_l.at[p])
        )

    with jax.named_scope("regroup"):
        pack_wide(*pairs[0], wide_s.at[0])
        pl.semaphore_wait(barrier, len(peers))
        send_wide(0)
        pack_rest(pairs, rest_s)
        flights.append(send_blocks(me, fl, rest_s, rest_r, sems_w.at[0, 3], sems_w.at[1, 3], sems_l.at[3]))
        pack_wide(*pairs[1], wide_s.at[1])
        send_wide(1)
        pack_wide(*pairs[2], wide_s.at[2])
    with jax.named_scope("gram"):
        kp[...] = nt(x[...], x[...])
        c_k = []
        for k in (1, 2, 3):
            c_k.append(fl.start(kp, kr.at[k - 1], sems_k.at[0, k - 1], sems_k.at[1, k - 1], me.at_x(k)))

    def partial(acc, send, i, value):
        acc[i] = value
        send[i] = value.astype(BF)

    with jax.named_scope("forward"):
        blocks_landed(flights[0])
        blocks_landed(flights[1])
        send_wide(2)
        unpack(0, wide_r.at[0], rest_r, w_gate, w_up)
        for i, w in enumerate((w_gate, w_up)):
            partial(acc_a, send_a, i, nn(x[...], w[...]))
        c_a = scatter_x(me, fl, send_a, slots_a, sems_a)
        blocks_landed(flights[2])
        unpack(1, wide_r.at[1], rest_r, s_gate, s_up)
        for i, w in enumerate((s_gate, s_up)):
            partial(acc_d, send_d, i, nn(x[...], w[...]))
        c_d = scatter_x(me, fl, send_d, slots_d, sems_d)
    my_rows = rows_of(me.x, TQ)
    with jax.named_scope("hidden"):
        landed(c_a)
        gate_pre, up_pre = add_x(acc_a, slots_a, my_rows, 0), add_x(acc_a, slots_a, my_rows, 1)
        val, slope, curve = gelu_parts(gate_pre)
        slope_up = slope * up_pre
        hh[0, my_rows, :] = (val * up_pre).astype(BF)
        mm[0, my_rows, :] = slope_up
        mm[1, my_rows, :] = val
        own[0] = slope
        own[1] = up_pre * curve
        landed(c_d)
        gate_dot, up_dot = add_x(acc_d, slots_d, my_rows, 0), add_x(acc_d, slots_d, my_rows, 1)
        hh[1, my_rows, :] = (mm[0, my_rows, :] * gate_dot + mm[1, my_rows, :] * up_dot).astype(BF)
        c_h = gather_x(me, fl, hh, sems_h)
        own[2] = gate_dot
        own[3] = up_dot

    def transposed(i, s):
        for b in range(DB // 128):
            cols = slice(b * 128, (b + 1) * 128)
            start_t[i, :, cols] = s[cols, :].astype(F32).T.astype(BF)

    with jax.named_scope("starts"):
        transposed(0, s_gate)
        transposed(1, s_up)
        landed(c_k)
        total = kp[...] + (kr[0] + kr[1] + kr[2])
        high = total.astype(BF)
        kpair[0] = high
        kpair[1] = (total - high.astype(F32)).astype(BF)
        landed(c_h)
        c_m = gather_x(me, fl, mm, sems_m)
        blocks_landed(flights[3])
        unpack(2, wide_r.at[2], rest_r, w_down, s_down)

    def out_post(total, rows, lanes):
        return ((total - target[rows, lanes].astype(F32)) / float(TOK)).astype(BF)

    def dot_post(total, rows, lanes):
        return (total / float(TOK)).astype(BF)

    def both(first, second, posts, finals, second_partial):
        first.cores()
        second_partial()
        second.cores()
        first.ys()
        second.ys()
        first.zs()
        second.zs()
        first.reduce(finals[0], posts[0])
        second.reduce(finals[1], posts[1])
        first.spread()
        second.spread()
        first.collect()

    ch_o = Chunk(me, fl, acc_o, send_o, (o0, o1, o2, o3, o4, o5), whole_low, 640, whole_back, 512)
    ch_p = Chunk(me, fl, acc_p, send_p, (p0, p1, p2, p3, p4, p5), whole_low, 640, whole_back, 512)
    with jax.named_scope("outputs"):
        ch_o.put(nt(hh[0], w_down[...]))
        both(
            ch_o,
            ch_p,
            (out_post, dot_post),
            (go, gd),
            lambda: ch_p.put(nt(hh[1], w_down[...]) + nt(hh[0], s_down[...])),
        )
    with jax.named_scope("back"):
        partial(acc_b, send_b, 0, nn(go[...], w_down[...]))
        c_b = scatter_x(me, fl, send_b, slots_b, sems_b)
        ch_p.collect()
        partial(acc_c, send_c, 0, nn(gd[...], w_down[...]) + nn(go[...], s_down[...]))
        c_c = scatter_x(me, fl, send_c, slots_c, sems_c)
        image = tn(hh[1], go[...]) + tn(hh[0], gd[...])
        one[2] = image
        u1d[...] = image.astype(BF)
        transposed(2, s_down)
        landed(c_b)
        grad_hidden = add_x(acc_b, slots_b, my_rows, 0)
        own[0] = grad_hidden * own[0]
        own[1] = grad_hidden * own[1]
        landed(c_c)
        back_dot = add_x(acc_c, slots_c, my_rows, 0)
        slope_term, curve_term = own[0], own[1]
        gu1[0, my_rows, :] = (
            back_dot * mm[0, my_rows, :] + slope_term * own[3] + curve_term * own[2]
        ).astype(BF)
        gu1[1, my_rows, :] = (back_dot * mm[1, my_rows, :] + slope_term * own[2]).astype(BF)
        c_g1 = gather_x(me, fl, gu1, sems_g1)
        landed(c_m)
        landed(c_g1)

    with jax.named_scope("second"):
        for i in range(2):
            tan2[i] = nn(kpair[0], gu1[i]) + nn(kpair[1], gu1[i])
        h2[...] = (mm[0] * tan2[0] + mm[1] * tan2[1]).astype(BF)
        ch_q = Chunk(me, fl, acc_o, send_o, (q0, q1, q2, q3, q4, q5), outer_low, 384, outer_low, 384)
        ch_r = Chunk(me, fl, acc_o, send_o, (r0, r1, r2, r3, r4, r5), inner_low, 256, inner_back, 128)
        for copy in ch_o.c1.values():
            copy.wait_send()
        done = [id(copy) for copy in ch_o.c1.values()]
        fl.sent = [copy for copy in fl.sent if id(copy) not in done]
        ch_q.put(nt(h2[...], w_down[...]) + nn(hh[0], u1d[...]))
        ch_q.cores()
        ch_r.cores()
        ch_q.ys()
        ch_r.ys()

    def dots_one(b, carry):
        rows = rows_of(b, BLK)
        ss, su, uu = carry
        for i in range(3):
            s = start_t[i, rows, :].astype(F32) * SCALE
            u = one[i, rows, :] * SCALE
            ss = ss + fold(s * s)
            su = su + fold(s * u)
            uu = uu + fold(u * u)
        return ss, su, uu

    zero = jnp.zeros((8, DB), F32)
    sum1 = ScalarSum(me, fl, sbuf1, ssem1)
    with jax.named_scope("image"):
        one[0] = tn(gu1[0], x[...])
        one[1] = tn(gu1[1], x[...])
        ch_q.zs()
        ch_r.zs()
        ss, su, uu = lax.fori_loop(0, HB // BLK, dots_one, (zero, zero, zero))
        ch_q.reduce(g2, dot_post)
        ch_r.reduce(g2, dot_post)
        sum1.go(0, tile_of([whole_sum(ss), whole_sum(su), whole_sum(uu)]))
        ch_q.spread()
        ch_r.spread()
        sum1.go(1, sum1.get())
        ch_q.collect()
        ch_r.collect()

    with jax.named_scope("back_second"):
        partial(acc_f, send_f, 0, nn(g2[...], w_down[...]) + nt(go[...], u1d[...]))
        c_f = scatter_x(me, fl, send_f, slots_f, sems_f)
        out_d[...] = tn(h2[...], go[...]) + tn(hh[0], g2[...])
        sum1.go(2, sum1.get())
        landed(c_f)
        back_dot = add_x(acc_f, slots_f, my_rows, 0)
        gate_two = tan2[0, my_rows, :]
        up_two = tan2[1, my_rows, :]
        gu2[0, my_rows, :] = (
            back_dot * mm[0, my_rows, :] + own[0] * up_two + own[1] * gate_two
        ).astype(BF)
        gu2[1, my_rows, :] = (back_dot * mm[1, my_rows, :] + own[0] * gate_two).astype(BF)
        c_g2 = gather_x(me, fl, gu2, sems_g2)
        norms = sum1.get() * (1.0 / (SCALE * SCALE * ENTRIES))
    s_s, s_u, u_u = norms[0:1, 0:1], norms[1:2, 0:1], norms[2:3, 0:1]
    f = 1.0 / jnp.sqrt(s_s + EPS)
    v11 = f * f * s_s
    h11 = f * f * s_u
    w11 = f * f * u_u
    rr = jnp.maximum(w11 - h11 * h11 * (2.0 - v11), 0.0)
    h21 = jnp.sqrt(rr + EPS)
    v12 = (h11 - h11 * v11) / h21
    v22 = rr / (h21 * h21)
    a1 = f / h21
    a0 = -h11 * f / h21

    def dots_two(b, carry):
        rows = rows_of(b, BLK)
        p1, p2, pw = carry
        s = start_t[2, rows, :].astype(F32)
        u = one[2, rows, :]
        w = (a1 * out_d[rows, :] + a0 * u) * SCALE
        first = f * s * SCALE
        second = (a1 * u + a0 * s) * SCALE
        return p1 + fold(first * w), p2 + fold(second * w), pw + fold(w * w)

    with jax.named_scope("last_dots"):
        d1, d2, dw = lax.fori_loop(0, HB // BLK, dots_two, (zero, zero, zero))
        d1, d2, dw = whole_sum(d1), whole_sum(d2), whole_sum(dw)
        for i in range(2):
            w = (
                a1 * gu2[i, my_rows, :].astype(F32) + a0 * gu1[i, my_rows, :].astype(F32)
            ) * SCALE
            first = own[2 + i]
            second = a1 * tan2[i, my_rows, :] + a0 * first
            d1 = d1 + whole_sum((f * SCALE) * first * w)
            d2 = d2 + whole_sum(second * SCALE * w)
        sum2 = ScalarSum(me, fl, sbuf2, ssem2)
        sum2.go(0, tile_of([d1, d2, dw]))
        landed(c_g2)
        dw = jnp.zeros((1, 1), F32)
        for i in range(2):
            w = (a1 * gu2[i].astype(F32) + a0 * gu1[i].astype(F32)) * SCALE
            high = w.astype(BF)
            low = (w - high.astype(F32)).astype(BF)
            kw = nn(kpair[0], high) + nn(kpair[1], high) + nn(kpair[0], low)
            dw = dw + whole_sum(w * kw)
        blank = jnp.zeros((1, 1), F32)
        sum2.go(1, sum2.get() + tile_of([blank, blank, dw]))
        out_g[...] = tn(gu2[0], x[...])
        sum2.go(2, sum2.get())
        out_u[...] = tn(gu2[1], x[...])
        norms = sum2.get() * (1.0 / (SCALE * SCALE * ENTRIES))
    h12, h22, ww = norms[0:1, 0:1], norms[1:2, 0:1], norms[2:3, 0:1]
    rr = (
        ww
        - 2.0 * (h12 * h12 + h22 * h22)
        + h12 * h12 * v11
        + h22 * h22 * v22
        + 2.0 * h12 * h22 * v12
    )
    h32 = jnp.sqrt(jnp.maximum(rr, 0.0) + EPS)
    c2 = a1 / h32
    c1 = (a0 - h22 * a1) / h32
    c0 = -(h12 * f + h22 * a0) / h32
    for i, value in enumerate((h21, h12, h22, h32)):
        hess[i] = jnp.max(value)
    ray[0] = jnp.max(h11)

    def third(b, carry):
        rows = rows_of(b, BLK)
        for i in range(3):
            twos[i][rows, :] = (
                c2 * twos[i][rows, :] + c1 * one[i, rows, :] + c0 * start_t[i, rows, :].astype(F32)
            )
        return carry

    with jax.named_scope("third"):
        lax.fori_loop(0, HB // BLK, third, 0)

    for copy in fl.sent:
        copy.wait_send()
    for chunk in (ch_o, ch_p, ch_q, ch_r):
        chunk.drain()


def rounds(*operands):
    dma = pltpu.SemaphoreType.DMA

    def xround(n):
        return [pltpu.VMEM((n, TOK, HB), F32), pltpu.VMEM((n, TOK, HB), BF), pltpu.VMEM((3, n, TQ, HB), BF), dma((2, 3))]

    scratch = (
        [pltpu.VMEM((3, NF, 2 * WR, WL), BF)] * 2
        + [pltpu.VMEM((NF, 2 * WR, 128), BF)] * 2
        + [dma((2, 4, NF)), dma((4,))]
        + [pltpu.VMEM((DB, HB), BF)] * 6
        + [pltpu.VMEM((3, HB, DB), BF), pltpu.VMEM((3, HB, DB), F32)]
        + [pltpu.VMEM((TOK, TOK), F32), pltpu.VMEM((3, TOK, TOK), F32), pltpu.VMEM((2, TOK, TOK), BF), dma((2, 3))]
        + xround(2) + xround(2)
        + [pltpu.VMEM((4, TQ, HB), F32), pltpu.VMEM((2, TOK, HB), BF), dma((2, 3)), pltpu.VMEM((2, TOK, HB), F32), dma((2, 3))]
        + [pltpu.VMEM((TOK, DB), F32), pltpu.VMEM((TOK, DB), BF)] * 2
        + chunk_scratch(640) + chunk_scratch(640)
        + [pltpu.VMEM((TOK, DB), BF)] * 2
        + xround(1) + xround(1)
        + [pltpu.VMEM((2, TOK, HB), BF), dma((2, 3)), pltpu.VMEM((HB, DB), BF), pltpu.VMEM((2, TOK, HB), F32), pltpu.VMEM((TOK, HB), BF)]
        + chunk_scratch(384) + chunk_scratch(256)
        + [pltpu.VMEM((TOK, DB), BF)]
        + xround(1)
        + [pltpu.VMEM((2, TOK, HB), BF), dma((2, 3))]
        + [pltpu.VMEM((24, 8, 128), F32), dma((2, 24)), pltpu.VMEM((24, 8, 128), F32), dma((2, 24))]
    )
    wide = jax.ShapeDtypeStruct((HB, DB), F32)
    return pl.pallas_call(
        kernel,
        out_shape=(wide, wide, wide, jax.ShapeDtypeStruct((4,), F32), jax.ShapeDtypeStruct((1,), F32)),
        in_specs=[pl.BlockSpec(memory_space=pltpu.VMEM)] * 8,
        out_specs=[pl.BlockSpec(memory_space=pltpu.VMEM)] * 3 + [pl.BlockSpec(memory_space=pltpu.SMEM)] * 2,
        scratch_shapes=scratch,
        compiler_params=pltpu.CompilerParams(
            collective_id=0, has_side_effects=True, vmem_limit_bytes=60 * 1024 * 1024
        ),
        name="arnoldi",
    )(*operands)


def on_device(inputs, target, w_gate, w_up, w_down, start_gate, start_up, start_down):
    third_g, third_u, third_d, hess, ray = rounds(
        inputs, target, w_gate, w_up, w_down.T, start_gate, start_up, start_down.T
    )
    return (
        third_g.T.reshape(DB, 1, HB),
        third_u.T.reshape(DB, 1, HB),
        third_d.reshape(1, HB, DB),
        hess,
        ray,
    )


def solution(mesh):
    placed = (
        P(None, "dcn"),
        P(None, "dcn"),
        P(("dcn", "fsdp"), "tp"),
        P(("dcn", "fsdp"), "tp"),
        P("tp", ("dcn", "fsdp")),
        P(("dcn", "fsdp"), "tp"),
        P(("dcn", "fsdp"), "tp"),
        P("tp", ("dcn", "fsdp")),
    )
    return jax.shard_map(
        on_device,
        mesh=mesh,
        in_specs=placed,
        out_specs=(
            P("dcn", "tp", "fsdp"),
            P("dcn", "tp", "fsdp"),
            P("tp", "fsdp", "dcn"),
            P(),
            P(),
        ),
        check_vma=False,
    )
```

```python
import math

import jax
import jax.numpy as jnp
from jax import lax
from jax.experimental import pallas as pl
from jax.experimental.pallas import tpu as pltpu
from jax.sharding import PartitionSpec as P

D = 4608
FF = 18432
TOK = 320
DB = 1152
HB = 288
TQ = 80
RQ = 16
NRED = 5
BLK = 48
NF = 16
WR = 72
WL = 256
SR = 24
BR = 176
ENTRIES = float(3 * D * FF)
EPS = 1e-06
SCALE = 2.0**-14
MESH = pl.DeviceIdType.MESH
BF = jnp.bfloat16
F32 = jnp.float32

gelu_cubic = 0.044715
gelu_scale = math.sqrt(2.0 / math.pi)


def gelu_parts(argument):
    squared = argument * argument
    inner_arg = gelu_scale * (argument + gelu_cubic * squared * argument)
    tanh_val = jnp.tanh(inner_arg)
    sech_square = 1.0 - tanh_val * tanh_val
    inner_slope = gelu_scale * (1.0 + 3.0 * gelu_cubic * squared)
    inner_curve = gelu_scale * 6.0 * gelu_cubic * argument
    gelu_val = 0.5 * argument * (1.0 + tanh_val)
    gelu_slope = 0.5 * (1.0 + tanh_val) + 0.5 * argument * sech_square * inner_slope
    gelu_curve = sech_square * inner_slope + 0.5 * argument * (
        sech_square * inner_curve - 2.0 * tanh_val * sech_square * inner_slope * inner_slope
    )
    return (gelu_val, gelu_slope, gelu_curve)


def nn(a, b):
    return lax.dot_general(a, b, (((1,), (0,)), ((), ())), preferred_element_type=F32)


def nt(a, b):
    return lax.dot_general(a, b, (((1,), (1,)), ((), ())), preferred_element_type=F32)


def tn(a, b):
    return lax.dot_general(a, b, (((0,), (0,)), ((), ())), preferred_element_type=F32)


class Place:
    def __init__(self):
        self.x = lax.axis_index("dcn")
        fsdp = lax.axis_index("fsdp")
        tp = lax.axis_index("tp")
        self.f = fsdp
        self.t = tp
        self.y = fsdp // 4
        self.half = (fsdp % 4) // 2
        self.m = self.y * 2 + fsdp % 2
        self.p = fsdp + 2 - 4 * self.half
        self.z = (tp // 2) * 4 + fsdp % 4
        self.c = tp % 2

    def dev(self, x=None, y=None, z=None, c=None):
        x = self.x if x is None else x
        y = self.y if y is None else y
        z = self.z if z is None else z
        c = self.c if c is None else c
        return (x, y * 4 + z % 4, (z // 4) * 2 + c)

    def at_x(self, k):
        return self.dev(x=(self.x + k) % 4)

    def at_y(self, k):
        return self.dev(y=(self.y + k) % 4)

    def at_z(self, k):
        return self.dev(z=(self.z + k) % 8)

    def at_f(self, k):
        return (self.x, (self.f + k) % NF, self.t)

    def near(self, k):
        m = (self.m + k) % 8
        f = (m // 2) * 4 + self.half * 2 + m % 2
        return f, f + 2 - 4 * self.half

    def partner(self):
        return (self.x, self.p, self.t)

    def at_t(self, k):
        return (self.x, self.f, (self.t + k) % 4)

    def across(self, low):
        return self.dev(z=(1 - self.z // 4) * 4 + low)

    def other(self):
        return self.dev(c=1 - self.c)


def rows_of(index, size):
    return pl.ds(pl.multiple_of(index * size, size), size)


def lanes_at(start, size):
    return pl.ds(pl.multiple_of(start, 128), size)


def remote(src, dst, ssem, rsem, dev):
    return pltpu.make_async_remote_copy(
        src_ref=src, dst_ref=dst, send_sem=ssem, recv_sem=rsem, device_id=dev, device_id_type=MESH
    )


class Flight:
    def __init__(self):
        self.sent = []

    def start(self, src, dst, ssem, rsem, dev):
        copy = remote(src, dst, ssem, rsem, dev)
        copy.start()
        self.sent.append(copy)
        return copy


def pack(first, second, out):
    lane = lax.broadcasted_iota(jnp.int32, (SR, 128), 1)
    for j in range(NF):
        lanes = slice(j * HB, j * HB + WL)
        wide = jnp.concatenate([first[:, lanes].astype(F32), second[:, lanes].astype(F32)], axis=0)
        start = j * HB + WL
        base = start - start % 128
        both = jnp.concatenate(
            [first[:, base : base + 128].astype(F32), second[:, base : base + 128].astype(F32)], axis=0
        )
        tiles = []
        for group in ((0, 1, 2, 3), (4, 5)):
            tile = jnp.zeros((SR, 128), F32)
            for g in group:
                strip = both[g * SR : (g + 1) * SR]
                at = (32 * g) % 128
                shift = (at - start) % 128
                if shift:
                    strip = pltpu.roll(strip, shift, axis=1)
                tile = jnp.where((lane >= at) & (lane < at + 32), strip, tile)
            tiles.append(tile)
        rest = jnp.concatenate(tiles, axis=1)
        blank = jnp.zeros((BR - 2 * WR - SR, WL), F32)
        out[j] = jnp.concatenate([wide, rest, blank], axis=0).astype(BF)


def unpack(a, b, first, second, rows):
    a, b = a[...].astype(F32), b[...].astype(F32)
    rests = []
    for v in (a, b):
        strips = []
        for g in range(6):
            at = 32 * g
            tile = v[2 * WR : 2 * WR + SR, at - at % 128 : at - at % 128 + 128]
            if at % 128:
                tile = pltpu.roll(tile, 128 - at % 128, axis=1)
            strips.append(tile)
        rests.append(jnp.concatenate(strips, axis=0))
    first[rows, 0:WL] = jnp.concatenate([a[:WR], b[:WR]], axis=0).astype(BF)
    second[rows, 0:WL] = jnp.concatenate([a[WR : 2 * WR], b[WR : 2 * WR]], axis=0).astype(BF)
    a, b = rests
    first[rows, WL:HB] = jnp.concatenate([a[:WR], b[:WR]], axis=0)[:, 0:32].astype(BF)
    second[rows, WL:HB] = jnp.concatenate([a[WR:], b[WR:]], axis=0)[:, 0:32].astype(BF)


def unpack_half(half, blocks, first, second):
    for y in range(4):
        rows = pl.ds(pl.multiple_of(y * 4 * WR + half * 2 * WR, 2 * WR), 2 * WR)
        unpack(blocks.at[2 * y], blocks.at[2 * y + 1], first, second, rows)


def send_blocks(me, fl, out, land, sems, lsem):
    copies = []
    for k in range(1, NF):
        copies.append(
            fl.start(out.at[(me.f + k) % NF], land.at[me.f], sems.at[0, k], sems.at[1, k], me.at_f(k))
        )
    own = pltpu.make_async_copy(out.at[me.f], land.at[me.f], lsem)
    own.start()
    return copies, (own,)


def send_near(me, fl, out, land, sems, lsems):
    copies = []
    for k in range(1, 8):
        f, p = me.near(k)
        for q, j in enumerate((f, p)):
            copies.append(
                fl.start(
                    out.at[j], land.at[q, me.m], sems.at[0, q, k], sems.at[1, q, k], (me.x, f, me.t)
                )
            )
    own = []
    for q, j in enumerate((me.f, me.p)):
        own.append(pltpu.make_async_copy(out.at[j], land.at[q, me.m], lsems.at[q]))
        own[-1].start()
    return copies, own


def blocks_landed(flight):
    landed(flight[0])
    for copy in flight[1]:
        copy.wait()


def scatter_x(me, fl, stage, slots, sems):
    out = []
    for k in (1, 2, 3):
        peer = (me.x + k) % 4
        out.append(
            fl.start(
                stage.at[:, rows_of(peer, TQ), :],
                slots.at[k - 1],
                sems.at[0, k - 1],
                sems.at[1, k - 1],
                me.at_x(k),
            )
        )
    return out


def gather_x(me, fl, buf, sems):
    out = []
    mine = buf.at[:, rows_of(me.x, TQ), :]
    for k in (1, 2, 3):
        out.append(fl.start(mine, mine, sems.at[0, k - 1], sems.at[1, k - 1], me.at_x(k)))
    return out


def landed(copies):
    for copy in copies:
        copy.wait_recv()


class Chunk:
    def __init__(self, me, fl, acc, send, scratch, low, width, back, back_width):
        self.me, self.fl, self.acc, self.send = me, fl, acc, send
        (self.r1, self.t1b, self.r2, self.t2b, self.r3, self.sems) = scratch
        self.mine = lanes_at(low(me.c), width)
        self.theirs = lanes_at(low(1 - me.c), width)
        self.back = lanes_at(back(me.c), back_width)

    def go(self, src, dst, sem, dev, rsem=None):
        return self.fl.start(src, dst, self.sems.at[0, sem], self.sems.at[1, sem], dev)

    def put(self, value):
        self.acc[...] = value
        self.send[...] = value.astype(BF)

    def cores(self):
        me = self.me
        self.c1 = {}
        for k in (1, 2, 3, 0):
            rows = rows_of((me.y + k) % 4, TQ)
            self.c1[k] = self.go(self.send.at[rows, self.theirs], self.r1.at[rows, :], k, me.other())

    def ys(self):
        me = self.me
        self.c2 = []
        for k in (1, 2, 3):
            landed([self.c1[k]])
            rows = rows_of((me.y + k) % 4, TQ)
            self.t1b[rows, :] = (self.acc[rows, self.mine] + self.r1[rows, :].astype(F32)).astype(BF)
            self.c2.append(self.go(self.t1b.at[rows, :], self.r2.at[k - 1], 3 + k, me.at_y(k)))

    def zs(self):
        me = self.me
        landed([self.c1[0]])
        rows = rows_of(me.y, TQ)
        total = self.acc[rows, self.mine] + self.r1[rows, :].astype(F32)
        landed(self.c2)
        for k in range(3):
            total = total + self.r2[k].astype(F32)
        self.t2b[...] = total.astype(BF)
        for q in range(NRED):

            @pl.when(me.z != q)
            def _():
                remote(
                    self.t2b.at[q * RQ : (q + 1) * RQ, :],
                    self.r3.at[me.z],
                    self.sems.at[0, 7 + q],
                    self.sems.at[1, 7 + me.z],
                    me.dev(z=q),
                ).start()

    def reduce(self, final, post):
        me = self.me
        self.final = final

        @pl.when(me.z < NRED)
        def _():
            self.r3[me.z] = self.t2b[rows_of(me.z, RQ), :]
            for s in range(8):

                @pl.when(me.z != s)
                def _():
                    remote(
                        self.t2b.at[0:RQ, :],
                        self.r3.at[s],
                        self.sems.at[0, 7],
                        self.sems.at[1, 7 + s],
                        me.other(),
                    ).wait_recv()

            rows = pl.ds(pl.multiple_of(me.y * TQ + me.z * RQ, RQ), RQ)
            total = self.r3[0].astype(F32)
            for s in range(1, 8):
                total = total + self.r3[s].astype(F32)
            final[rows, self.mine] = post(total, rows, self.mine)
            for k in range(1, 8):
                piece = final.at[rows, self.mine]
                remote(
                    piece, piece, self.sems.at[0, 14 + k], self.sems.at[1, 15 + me.z], me.at_z(k)
                ).start()

    def spread(self):
        me, final = self.me, self.final
        for q in range(NRED):
            piece = final.at[pl.ds(pl.multiple_of(me.y * TQ + q * RQ, RQ), RQ), self.mine]

            @pl.when(me.z != q)
            def _():
                remote(piece, piece, self.sems.at[0, 7], self.sems.at[1, 15 + q], me.other()).wait_recv()

        rows = rows_of(me.y, TQ)
        block = final.at[rows, self.mine]
        self.c5 = [self.go(block, block, 21 + k, me.at_y(k)) for k in (1, 2, 3)]
        block = final.at[rows, self.back]
        self.c6 = [self.go(block, block, 25, me.other())]

    def collect(self):
        me, final = self.me, self.final
        for k in (1, 2, 3):
            landed([self.c5[k - 1]])
            block = final.at[rows_of((me.y + 4 - k) % 4, TQ), self.back]
            self.c6.append(self.go(block, block, 25 + k, me.other()))
        landed(self.c6)

    def drain(self):
        me = self.me
        for q in range(NRED):

            @pl.when(me.z != q)
            def _():
                remote(
                    self.t2b.at[q * RQ : (q + 1) * RQ, :],
                    self.r3.at[me.z],
                    self.sems.at[0, 7 + q],
                    self.sems.at[1, 7 + me.z],
                    me.dev(z=q),
                ).wait_send()

        @pl.when(me.z < NRED)
        def _():
            for k in range(1, 8):
                remote(
                    self.t2b.at[0:RQ, :],
                    self.t2b.at[0:RQ, :],
                    self.sems.at[0, 14 + k],
                    self.sems.at[1, 15],
                    me.other(),
                ).wait_send()


def chunk_scratch(width):
    return [
        pltpu.VMEM((TOK, width), BF),
        pltpu.VMEM((TOK, width), BF),
        pltpu.VMEM((3, TQ, width), BF),
        pltpu.VMEM((TQ, width), BF),
        pltpu.VMEM((8, RQ, width), BF),
        pltpu.SemaphoreType.DMA((2, 30)),
    ]


class ScalarSum:
    def __init__(self, me, fl, buf, sems):
        self.me, self.fl, self.buf, self.sems = me, fl, buf, sems

    def go(self, stage, tile):
        me = self.me
        index, base, count, at = (
            (me.x, 0, 4, me.at_x),
            (me.f, 4, 16, me.at_f),
            (me.t, 20, 4, me.at_t),
        )[stage]
        mine = self.buf.at[base + index]
        self.buf[base + index] = tile
        self.copies = []
        for k in range(1, count):
            self.copies.append(
                self.fl.start(mine, mine, self.sems.at[0, base + k], self.sems.at[1, base + k], at(k))
            )
        self.span = (base, count)

    def get(self):
        landed(self.copies)
        base, count = self.span
        total = self.buf[base]
        for s in range(1, count):
            total = total + self.buf[base + s]
        return total


def whole_sum(value):
    return jnp.sum(jnp.sum(value, axis=1, keepdims=True), axis=0, keepdims=True)


def fold(value):
    return jnp.sum(value.reshape(BLK // 8, 8, DB), axis=0)


def tile_of(values):
    rows = [jnp.broadcast_to(v, (1, 128)) for v in values]
    while len(rows) < 8:
        rows.append(jnp.zeros((1, 128), F32))
    return jnp.concatenate(rows, axis=0)


def add_x(send, slots, rows, i):
    total = send[i, rows, :].astype(F32)
    for k in range(3):
        total = total + slots[k, i].astype(F32)
    return total


def whole_low(c):
    return c * 512


def whole_back(c):
    return c * 640


def outer_low(c):
    return c * 768


def inner_low(c):
    return 384 + c * 128


def inner_back(c):
    return 384 + c * 256


def kernel(
    x, target, in_wg, in_wu, in_wd, in_sg, in_su, in_sd,
    out_g, out_u, out_d, hess, ray,
    out_w, near_r, full_r, far_r, sems_w, sems_n, sems_l, sems_p,
    parts, w_down, s_down, start_t, one, cross_s, cross_r,
    kp, kr, kpair, sems_k,
    send_a, slots_a, sems_a, send_d, slots_d, sems_d,
    own, hh, sems_h, mm, sems_m,
    acc_o, send_o, acc_p, send_p,
    o0, o1, o2, o3, o4, o5, p0, p1, p2, p3, p4, p5,
    go, gd,
    send_b, slots_b, sems_b, send_c, slots_c, sems_c,
    gu1, sems_g1, u1d, tan2, h2,
    q0, q1, q2, q3, q4, q5, r0, r1, r2, r3, r4, r5,
    g2,
    send_f, slots_f, sems_f,
    gu2, sems_g2,
    sbuf1, ssem1, sbuf2, ssem2,
):
    me = Place()
    fl = Flight()
    twos = (out_g, out_u, out_d)

    barrier = pltpu.get_barrier_semaphore()
    peers = (
        [me.at_f(k) for k in range(1, NF)]
        + [me.at_t(k) for k in (1, 2, 3)]
        + [me.at_x(k) for k in (1, 2, 3)]
        + [me.across(low) for low in range(4)]
    )
    for peer in peers:
        pl.semaphore_signal(barrier, inc=1, device_id=peer, device_id_type=MESH)

    pairs = ((in_wg, in_wu), (in_sg, in_su), (in_wd, in_sd))
    flights = []

    with jax.named_scope("regroup"):
        pack(*pairs[0], out_w.at[0])
        pl.semaphore_wait(barrier, len(peers))
        flights.append(send_near(me, fl, out_w.at[0], near_r.at[0], sems_n.at[0], sems_l.at[0]))
        pack(*pairs[1], out_w.at[1])
        flights.append(send_near(me, fl, out_w.at[1], near_r.at[1], sems_n.at[1], sems_l.at[1]))
        pack(*pairs[2], out_w.at[2])
        parts[...] = jnp.zeros(parts.shape, BF)

    def squares(b, total):
        rows = pl.ds(pl.multiple_of(b * 8, 8), 8)
        for ref in (in_sg, in_su, in_sd):
            v = ref[rows, :].astype(F32) * SCALE
            total = total + v * v
        return total

    with jax.named_scope("gram"):
        kp[...] = nt(x[...], x[...])
        c_k = []
        for k in (1, 2, 3):
            c_k.append(fl.start(kp, kr.at[k - 1], sems_k.at[0, k - 1], sems_k.at[1, k - 1], me.at_x(k)))
        start_square = lax.fori_loop(0, WR // 8, squares, jnp.zeros((8, FF // 4), F32))
        start_square = whole_sum(start_square)

    def partial(send, i, value):
        send[i] = value.astype(BF)

    my_rows = rows_of(me.x, TQ)

    def forward(p, send, slots, sems):
        for q in range(2):
            unpack_half(me.half, near_r.at[p, q], parts.at[q, 2 * p], parts.at[q, 2 * p + 1])
            for i in range(2):
                partial(send, 2 * q + i, nn(x[...], parts[q, 2 * p + i]))
        return scatter_x(me, fl, send, slots, sems)

    def cross(p, send, slots):
        for i in range(2):
            cross_s[p, i] = add_x(send, slots, my_rows, 2 + i).astype(BF)
        return fl.start(cross_s.at[p], cross_r.at[p], sems_p.at[0, p], sems_p.at[1, p], me.partner())

    def joined(p, send, slots, i):
        return add_x(send, slots, my_rows, i) + cross_r[p, i].astype(F32)

    with jax.named_scope("forward"):
        blocks_landed(flights[0])
        flights.append(send_blocks(me, fl, out_w.at[2], full_r, sems_w, sems_l.at[2, 0]))
        c_a = forward(0, send_a, slots_a, sems_a)
        blocks_landed(flights[1])
        c_d = forward(1, send_d, slots_d, sems_d)
        landed(c_a)
        cross_a = cross(0, send_a, slots_a)
    with jax.named_scope("hidden"):
        landed([cross_a])
        gate_pre, up_pre = joined(0, send_a, slots_a, 0), joined(0, send_a, slots_a, 1)
        val, slope, curve = gelu_parts(gate_pre)
        slope_up = slope * up_pre
        hh[0, my_rows, :] = (val * up_pre).astype(BF)
        mm[0, my_rows, :] = slope_up
        mm[1, my_rows, :] = val
        own[0] = slope
        own[1] = up_pre * curve
        landed(c_d)
        cross_d = cross(1, send_d, slots_d)
        landed([cross_d])
        gate_dot, up_dot = joined(1, send_d, slots_d, 0), joined(1, send_d, slots_d, 1)
        hh[1, my_rows, :] = (mm[0, my_rows, :] * gate_dot + mm[1, my_rows, :] * up_dot).astype(BF)
        c_h = gather_x(me, fl, hh, sems_h)
        own[2] = gate_dot
        own[3] = up_dot

    def transposed(i, s):
        for b in range(DB // 128):
            cols = slice(b * 128, (b + 1) * 128)
            start_t[i, :, cols] = s[cols, :].astype(F32).T.astype(BF)

    with jax.named_scope("starts"):
        landed(c_h)
        c_m = gather_x(me, fl, mm, sems_m)
        blocks_landed(flights[2])
        for i in range(NF // 2):
            rows = slice(i * 2 * WR, (i + 1) * 2 * WR)
            unpack(full_r.at[2 * i], full_r.at[2 * i + 1], w_down, s_down, rows)

    def far(part):
        blocks = pl.ds(part * 4, 4)
        return fl.start(
            near_r.at[1, 1, blocks], far_r.at[blocks], sems_p.at[0, 2 + part], sems_p.at[1, 2 + part], me.partner()
        )

    def out_post(total, rows, lanes):
        return ((total - target[rows, lanes].astype(F32)) / float(TOK)).astype(BF)

    def dot_post(total, rows, lanes):
        return (total / float(TOK)).astype(BF)

    def both(first, second, posts, finals, second_partial):
        first.cores()
        second_partial()
        second.cores()
        first.ys()
        second.ys()
        first.zs()
        second.zs()
        first.reduce(finals[0], posts[0])
        second.reduce(finals[1], posts[1])
        first.spread()
        second.spread()
        first.collect()

    ch_o = Chunk(me, fl, acc_o, send_o, (o0, o1, o2, o3, o4, o5), whole_low, 640, whole_back, 512)
    ch_p = Chunk(me, fl, acc_p, send_p, (p0, p1, p2, p3, p4, p5), whole_low, 640, whole_back, 512)
    with jax.named_scope("outputs"):
        ch_o.put(nt(hh[0], w_down[...]))
        both(
            ch_o,
            ch_p,
            (out_post, dot_post),
            (go, gd),
            lambda: ch_p.put(nt(hh[1], w_down[...]) + nt(hh[0], s_down[...])),
        )
    with jax.named_scope("back"):
        partial(send_b, 0, nn(go[...], w_down[...]))
        c_b = scatter_x(me, fl, send_b, slots_b, sems_b)
        c_far = [far(0)]
        ch_p.collect()
        partial(send_c, 0, nn(gd[...], w_down[...]) + nn(go[...], s_down[...]))
        c_c = scatter_x(me, fl, send_c, slots_c, sems_c)
        image = tn(hh[1], go[...]) + tn(hh[0], gd[...])
        one[2] = image
        u1d[...] = image.astype(BF)
        transposed(2, s_down)
        landed(c_b)
        grad_hidden = add_x(send_b, slots_b, my_rows, 0)
        own[0] = grad_hidden * own[0]
        own[1] = grad_hidden * own[1]
        landed(c_c)
        back_dot = add_x(send_c, slots_c, my_rows, 0)
        slope_term, curve_term = own[0], own[1]
        gu1[0, my_rows, :] = (
            back_dot * mm[0, my_rows, :] + slope_term * own[3] + curve_term * own[2]
        ).astype(BF)
        gu1[1, my_rows, :] = (back_dot * mm[1, my_rows, :] + slope_term * own[2]).astype(BF)
        c_g1 = gather_x(me, fl, gu1, sems_g1)
        landed(c_m)
        landed(c_k)
        total = kp[...] + (kr[0] + kr[1] + kr[2])
        high = total.astype(BF)
        kpair[0] = high
        kpair[1] = (total - high.astype(F32)).astype(BF)
        landed(c_g1)

    with jax.named_scope("second"):
        for i in range(2):
            tan2[i] = nn(kpair[0], gu1[i]) + nn(kpair[1], gu1[i])
        h2[...] = (mm[0] * tan2[0] + mm[1] * tan2[1]).astype(BF)
        ch_q = Chunk(me, fl, acc_o, send_o, (q0, q1, q2, q3, q4, q5), outer_low, 384, outer_low, 384)
        ch_r = Chunk(me, fl, acc_o, send_o, (r0, r1, r2, r3, r4, r5), inner_low, 256, inner_back, 128)
        for copy in ch_o.c1.values():
            copy.wait_send()
        done = [id(copy) for copy in ch_o.c1.values()]
        fl.sent = [copy for copy in fl.sent if id(copy) not in done]
        ch_q.put(nt(h2[...], w_down[...]) + nn(hh[0], u1d[...]))
        ch_q.cores()
        ch_r.cores()
        ch_q.ys()
        ch_r.ys()

    def dots_one(b, carry):
        rows = rows_of(b, BLK)
        su, uu = carry
        s = start_t[2, rows, :].astype(F32) * SCALE
        u = one[2, rows, :] * SCALE
        return su + fold(s * u), uu + fold(u * u)

    zero = jnp.zeros((8, DB), F32)
    sum1 = ScalarSum(me, fl, sbuf1, ssem1)
    with jax.named_scope("image"):
        one[0] = tn(gu1[0], x[...])
        one[1] = tn(gu1[1], x[...])
        ch_q.zs()
        ch_r.zs()
        su, uu = lax.fori_loop(0, HB // BLK, dots_one, (zero, zero))
        su, uu = whole_sum(su), whole_sum(uu)
        for i in range(2):
            g = gu1[i, my_rows, :].astype(F32) * SCALE
            su = su + whole_sum(own[2 + i] * SCALE * g)
            uu = uu + whole_sum(tan2[i, my_rows, :] * SCALE * g)
        ch_q.reduce(g2, dot_post)
        ch_r.reduce(g2, dot_post)
        sum1.go(0, tile_of([start_square, su, uu]))
        ch_q.spread()
        ch_r.spread()
        sum1.go(1, sum1.get())
        ch_q.collect()
        ch_r.collect()

    with jax.named_scope("back_second"):
        partial(send_f, 0, nn(g2[...], w_down[...]) + nt(go[...], u1d[...]))
        c_f = scatter_x(me, fl, send_f, slots_f, sems_f)
        c_far.append(far(1))
        out_d[...] = tn(h2[...], go[...]) + tn(hh[0], g2[...])
        sum1.go(2, sum1.get())
        landed(c_f)
        back_dot = add_x(send_f, slots_f, my_rows, 0)
        gate_two = tan2[0, my_rows, :]
        up_two = tan2[1, my_rows, :]
        gu2[0, my_rows, :] = (
            back_dot * mm[0, my_rows, :] + own[0] * up_two + own[1] * gate_two
        ).astype(BF)
        gu2[1, my_rows, :] = (back_dot * mm[1, my_rows, :] + own[0] * gate_two).astype(BF)
        c_g2 = gather_x(me, fl, gu2, sems_g2)
        norms = sum1.get() * (1.0 / (SCALE * SCALE * ENTRIES))
    s_s, s_u, u_u = norms[0:1, 0:1], norms[1:2, 0:1], norms[2:3, 0:1]
    f = 1.0 / jnp.sqrt(s_s + EPS)
    v11 = f * f * s_s
    h11 = f * f * s_u
    w11 = f * f * u_u
    rr = jnp.maximum(w11 - h11 * h11 * (2.0 - v11), 0.0)
    h21 = jnp.sqrt(rr + EPS)
    v12 = (h11 - h11 * v11) / h21
    v22 = rr / (h21 * h21)
    a1 = f / h21
    a0 = -h11 * f / h21

    def dots_two(b, carry):
        rows = rows_of(b, BLK)
        p1, p2, pw = carry
        s = start_t[2, rows, :].astype(F32)
        u = one[2, rows, :]
        w = (a1 * out_d[rows, :] + a0 * u) * SCALE
        first = f * s * SCALE
        second = (a1 * u + a0 * s) * SCALE
        return p1 + fold(first * w), p2 + fold(second * w), pw + fold(w * w)

    with jax.named_scope("last_dots"):
        d1, d2, dw = lax.fori_loop(0, HB // BLK, dots_two, (zero, zero, zero))
        d1, d2, dw = whole_sum(d1), whole_sum(d2), whole_sum(dw)
        for i in range(2):
            w = (
                a1 * gu2[i, my_rows, :].astype(F32) + a0 * gu1[i, my_rows, :].astype(F32)
            ) * SCALE
            first = own[2 + i]
            second = a1 * tan2[i, my_rows, :] + a0 * first
            d1 = d1 + whole_sum((f * SCALE) * first * w)
            d2 = d2 + whole_sum(second * SCALE * w)
        sum2 = ScalarSum(me, fl, sbuf2, ssem2)
        sum2.go(0, tile_of([d1, d2, dw]))
        landed(c_g2)
        dw = jnp.zeros((1, 1), F32)
        for i in range(2):
            w = (a1 * gu2[i].astype(F32) + a0 * gu1[i].astype(F32)) * SCALE
            high = w.astype(BF)
            low = (w - high.astype(F32)).astype(BF)
            kw = nn(kpair[0], high) + nn(kpair[1], high) + nn(kpair[0], low)
            dw = dw + whole_sum(w * kw)
        blank = jnp.zeros((1, 1), F32)
        sum2.go(1, sum2.get() + tile_of([blank, blank, dw]))
        out_g[...] = tn(gu2[0], x[...])
        sum2.go(2, sum2.get())
        out_u[...] = tn(gu2[1], x[...])
        landed(c_far)
        unpack_half(1 - me.half, far_r, parts.at[0, 2], parts.at[0, 3])
        transposed(0, parts.at[0, 2])
        transposed(1, parts.at[0, 3])
        norms = sum2.get() * (1.0 / (SCALE * SCALE * ENTRIES))
    h12, h22, ww = norms[0:1, 0:1], norms[1:2, 0:1], norms[2:3, 0:1]
    rr = (
        ww
        - 2.0 * (h12 * h12 + h22 * h22)
        + h12 * h12 * v11
        + h22 * h22 * v22
        + 2.0 * h12 * h22 * v12
    )
    h32 = jnp.sqrt(jnp.maximum(rr, 0.0) + EPS)
    c2 = a1 / h32
    c1 = (a0 - h22 * a1) / h32
    c0 = -(h12 * f + h22 * a0) / h32
    for i, value in enumerate((h21, h12, h22, h32)):
        hess[i] = jnp.max(value)
    ray[0] = jnp.max(h11)

    def third(b, carry):
        rows = rows_of(b, BLK)
        for i in range(3):
            twos[i][rows, :] = (
                c2 * twos[i][rows, :] + c1 * one[i, rows, :] + c0 * start_t[i, rows, :].astype(F32)
            )
        return carry

    with jax.named_scope("third"):
        lax.fori_loop(0, HB // BLK, third, 0)

    for copy in fl.sent:
        copy.wait_send()
    for chunk in (ch_o, ch_p, ch_q, ch_r):
        chunk.drain()


def rounds(*operands):
    dma = pltpu.SemaphoreType.DMA

    def xround(n):
        return [pltpu.VMEM((n, TOK, HB), BF), pltpu.VMEM((3, n, TQ, HB), BF), dma((2, 3))]

    scratch = (
        [pltpu.VMEM((3, NF, BR, WL), BF), pltpu.VMEM((2, 2, 8, BR, WL), BF), pltpu.VMEM((NF, BR, WL), BF), pltpu.VMEM((8, BR, WL), BF)]
        + [dma((2, NF)), dma((2, 2, 2, 8)), dma((3, 2)), dma((2, 4))]
        + [pltpu.VMEM((2, 4, DB, HB), BF)] + [pltpu.VMEM((DB, HB), BF)] * 2
        + [pltpu.VMEM((3, HB, DB), BF), pltpu.VMEM((3, HB, DB), F32)] + [pltpu.VMEM((2, 2, TQ, HB), BF)] * 2
        + [pltpu.VMEM((TOK, TOK), F32), pltpu.VMEM((3, TOK, TOK), F32), pltpu.VMEM((2, TOK, TOK), BF), dma((2, 3))]
        + xround(4) + xround(4)
        + [pltpu.VMEM((4, TQ, HB), F32), pltpu.VMEM((2, TOK, HB), BF), dma((2, 3)), pltpu.VMEM((2, TOK, HB), F32), dma((2, 3))]
        + [pltpu.VMEM((TOK, DB), F32), pltpu.VMEM((TOK, DB), BF)] * 2
        + chunk_scratch(640) + chunk_scratch(640)
        + [pltpu.VMEM((TOK, DB), BF)] * 2
        + xround(1) + xround(1)
        + [pltpu.VMEM((2, TOK, HB), BF), dma((2, 3)), pltpu.VMEM((HB, DB), BF), pltpu.VMEM((2, TOK, HB), F32), pltpu.VMEM((TOK, HB), BF)]
        + chunk_scratch(384) + chunk_scratch(256)
        + [pltpu.VMEM((TOK, DB), BF)]
        + xround(1)
        + [pltpu.VMEM((2, TOK, HB), BF), dma((2, 3))]
        + [pltpu.VMEM((24, 8, 128), F32), dma((2, 24)), pltpu.VMEM((24, 8, 128), F32), dma((2, 24))]
    )
    wide = jax.ShapeDtypeStruct((HB, DB), F32)
    return pl.pallas_call(
        kernel,
        out_shape=(wide, wide, wide, jax.ShapeDtypeStruct((4,), F32), jax.ShapeDtypeStruct((1,), F32)),
        in_specs=[pl.BlockSpec(memory_space=pltpu.VMEM)] * 8,
        out_specs=[pl.BlockSpec(memory_space=pltpu.VMEM)] * 3 + [pl.BlockSpec(memory_space=pltpu.SMEM)] * 2,
        scratch_shapes=scratch,
        compiler_params=pltpu.CompilerParams(
            collective_id=0, has_side_effects=True, vmem_limit_bytes=60 * 1024 * 1024
        ),
        name="arnoldi",
    )(*operands)


def on_device(inputs, target, w_gate, w_up, w_down, start_gate, start_up, start_down):
    third_g, third_u, third_d, hess, ray = rounds(
        inputs, target, w_gate, w_up, w_down.T, start_gate, start_up, start_down.T
    )
    return (
        third_g.T.reshape(DB, 1, HB),
        third_u.T.reshape(DB, 1, HB),
        third_d.reshape(1, HB, DB),
        hess,
        ray,
    )


def solution(mesh):
    placed = (
        P(None, "dcn"),
        P(None, "dcn"),
        P(("dcn", "fsdp"), "tp"),
        P(("dcn", "fsdp"), "tp"),
        P("tp", ("dcn", "fsdp")),
        P(("dcn", "fsdp"), "tp"),
        P(("dcn", "fsdp"), "tp"),
        P("tp", ("dcn", "fsdp")),
    )
    return jax.shard_map(
        on_device,
        mesh=mesh,
        in_specs=placed,
        out_specs=(
            P("dcn", "tp", "fsdp"),
            P("dcn", "tp", "fsdp"),
            P("tp", "fsdp", "dcn"),
            P(),
            P(),
        ),
        check_vma=False,
    )
```

```python
import math

import jax
import jax.numpy as jnp
from jax import lax
from jax.experimental import pallas as pl
from jax.experimental.pallas import tpu as pltpu
from jax.sharding import PartitionSpec as P

D = 4608
FF = 18432
TOK = 320
DB = 1152
HB = 288
TQ = 80
RQ = 16
NRED = 5
BLK = 48
NF = 16
WR = 72
WL = 256
SR = 24
BR = 176
ENTRIES = float(3 * D * FF)
EPS = 1e-06
SCALE = 2.0**-14
MESH = pl.DeviceIdType.MESH
BF = jnp.bfloat16
F32 = jnp.float32

gelu_cubic = 0.044715
gelu_scale = math.sqrt(2.0 / math.pi)


def gelu_parts(argument):
    squared = argument * argument
    inner_arg = gelu_scale * (argument + gelu_cubic * squared * argument)
    tanh_val = jnp.tanh(inner_arg)
    sech_square = 1.0 - tanh_val * tanh_val
    inner_slope = gelu_scale * (1.0 + 3.0 * gelu_cubic * squared)
    inner_curve = gelu_scale * 6.0 * gelu_cubic * argument
    gelu_val = 0.5 * argument * (1.0 + tanh_val)
    gelu_slope = 0.5 * (1.0 + tanh_val) + 0.5 * argument * sech_square * inner_slope
    gelu_curve = sech_square * inner_slope + 0.5 * argument * (
        sech_square * inner_curve - 2.0 * tanh_val * sech_square * inner_slope * inner_slope
    )
    return (gelu_val, gelu_slope, gelu_curve)


def nn(a, b):
    return lax.dot_general(a, b, (((1,), (0,)), ((), ())), preferred_element_type=F32)


def nt(a, b):
    return lax.dot_general(a, b, (((1,), (1,)), ((), ())), preferred_element_type=F32)


def tn(a, b):
    return lax.dot_general(a, b, (((0,), (0,)), ((), ())), preferred_element_type=F32)


class Place:
    def __init__(self):
        self.x = lax.axis_index("dcn")
        fsdp = lax.axis_index("fsdp")
        tp = lax.axis_index("tp")
        self.f = fsdp
        self.t = tp
        self.y = fsdp // 4
        self.half = (fsdp % 4) // 2
        self.m = self.y * 2 + fsdp % 2
        self.p = fsdp + 2 - 4 * self.half
        self.z = (tp // 2) * 4 + fsdp % 4
        self.c = tp % 2

    def dev(self, x=None, y=None, z=None, c=None):
        x = self.x if x is None else x
        y = self.y if y is None else y
        z = self.z if z is None else z
        c = self.c if c is None else c
        return (x, y * 4 + z % 4, (z // 4) * 2 + c)

    def at_x(self, k):
        return self.dev(x=(self.x + k) % 4)

    def at_y(self, k):
        return self.dev(y=(self.y + k) % 4)

    def at_z(self, k):
        return self.dev(z=(self.z + k) % 8)

    def at_f(self, k):
        return (self.x, (self.f + k) % NF, self.t)

    def near(self, k):
        m = (self.m + k) % 8
        f = (m // 2) * 4 + self.half * 2 + m % 2
        return f, f + 2 - 4 * self.half

    def partner(self):
        return (self.x, self.p, self.t)

    def at_t(self, k):
        return (self.x, self.f, (self.t + k) % 4)

    def across(self, low):
        return self.dev(z=(1 - self.z // 4) * 4 + low)

    def other(self):
        return self.dev(c=1 - self.c)


def rows_of(index, size):
    return pl.ds(pl.multiple_of(index * size, size), size)


def lanes_at(start, size):
    return pl.ds(pl.multiple_of(start, 128), size)


def remote(src, dst, ssem, rsem, dev):
    return pltpu.make_async_remote_copy(
        src_ref=src, dst_ref=dst, send_sem=ssem, recv_sem=rsem, device_id=dev, device_id_type=MESH
    )


class Flight:
    def __init__(self):
        self.sent = []

    def start(self, src, dst, ssem, rsem, dev):
        copy = remote(src, dst, ssem, rsem, dev)
        copy.start()
        self.sent.append(copy)
        return copy


def pack(first, second, out):
    lane = lax.broadcasted_iota(jnp.int32, (SR, 128), 1)
    for j in range(NF):
        lanes = slice(j * HB, j * HB + WL)
        wide = jnp.concatenate([first[:, lanes].astype(F32), second[:, lanes].astype(F32)], axis=0)
        start = j * HB + WL
        base = start - start % 128
        both = jnp.concatenate(
            [first[:, base : base + 128].astype(F32), second[:, base : base + 128].astype(F32)], axis=0
        )
        tiles = []
        for group in ((0, 1, 2, 3), (4, 5)):
            tile = jnp.zeros((SR, 128), F32)
            for g in group:
                strip = both[g * SR : (g + 1) * SR]
                at = (32 * g) % 128
                shift = (at - start) % 128
                if shift:
                    strip = pltpu.roll(strip, shift, axis=1)
                tile = jnp.where((lane >= at) & (lane < at + 32), strip, tile)
            tiles.append(tile)
        rest = jnp.concatenate(tiles, axis=1)
        blank = jnp.zeros((BR - 2 * WR - SR, WL), F32)
        out[j] = jnp.concatenate([wide, rest, blank], axis=0).astype(BF)


def unpack(a, b, first, second, rows):
    a, b = a[...].astype(F32), b[...].astype(F32)
    rests = []
    for v in (a, b):
        strips = []
        for g in range(6):
            at = 32 * g
            tile = v[2 * WR : 2 * WR + SR, at - at % 128 : at - at % 128 + 128]
            if at % 128:
                tile = pltpu.roll(tile, 128 - at % 128, axis=1)
            strips.append(tile)
        rests.append(jnp.concatenate(strips, axis=0))
    first[rows, 0:WL] = jnp.concatenate([a[:WR], b[:WR]], axis=0).astype(BF)
    second[rows, 0:WL] = jnp.concatenate([a[WR : 2 * WR], b[WR : 2 * WR]], axis=0).astype(BF)
    a, b = rests
    first[rows, WL:HB] = jnp.concatenate([a[:WR], b[:WR]], axis=0)[:, 0:32].astype(BF)
    second[rows, WL:HB] = jnp.concatenate([a[WR:], b[WR:]], axis=0)[:, 0:32].astype(BF)


def unpack_half(half, blocks, first, second):
    for y in range(4):
        rows = pl.ds(pl.multiple_of(y * 4 * WR + half * 2 * WR, 2 * WR), 2 * WR)
        unpack(blocks.at[2 * y], blocks.at[2 * y + 1], first, second, rows)


def send_blocks(me, fl, out, land, sems, lsem):
    copies = []
    for k in range(1, NF):
        copies.append(
            fl.start(out.at[(me.f + k) % NF], land.at[me.f], sems.at[0, k], sems.at[1, k], me.at_f(k))
        )
    own = pltpu.make_async_copy(out.at[me.f], land.at[me.f], lsem)
    own.start()
    return copies, (own,)


def send_near(me, fl, out, land, sems, lsems):
    copies = []
    for k in range(1, 8):
        f, p = me.near(k)
        for q, j in enumerate((f, p)):
            copies.append(
                fl.start(
                    out.at[j], land.at[q, me.m], sems.at[0, q, k], sems.at[1, q, k], (me.x, f, me.t)
                )
            )
    own = []
    for q, j in enumerate((me.f, me.p)):
        own.append(pltpu.make_async_copy(out.at[j], land.at[q, me.m], lsems.at[q]))
        own[-1].start()
    return copies, own


def blocks_landed(flight):
    landed(flight[0])
    for copy in flight[1]:
        copy.wait()


def scatter_x(me, fl, stage, slots, sems):
    out = []
    for k in (1, 2, 3):
        peer = (me.x + k) % 4
        out.append(
            fl.start(
                stage.at[:, rows_of(peer, TQ), :],
                slots.at[k - 1],
                sems.at[0, k - 1],
                sems.at[1, k - 1],
                me.at_x(k),
            )
        )
    return out


def gather_x(me, fl, buf, sems):
    out = []
    mine = buf.at[:, rows_of(me.x, TQ), :]
    for k in (1, 2, 3):
        out.append(fl.start(mine, mine, sems.at[0, k - 1], sems.at[1, k - 1], me.at_x(k)))
    return out


def landed(copies):
    for copy in copies:
        copy.wait_recv()


class Chunk:
    def __init__(self, me, fl, acc, send, scratch, low, width, back, back_width):
        self.me, self.fl, self.acc, self.send = me, fl, acc, send
        (self.r1, self.t1b, self.r2, self.t2b, self.r3, self.sems) = scratch
        self.mine = lanes_at(low(me.c), width)
        self.theirs = lanes_at(low(1 - me.c), width)
        self.back = lanes_at(back(me.c), back_width)

    def go(self, src, dst, sem, dev, rsem=None):
        return self.fl.start(src, dst, self.sems.at[0, sem], self.sems.at[1, sem], dev)

    def put(self, value):
        self.acc[...] = value
        self.send[...] = value.astype(BF)

    def cores(self):
        me = self.me
        self.c1 = {}
        for k in (1, 2, 3, 0):
            rows = rows_of((me.y + k) % 4, TQ)
            self.c1[k] = self.go(self.send.at[rows, self.theirs], self.r1.at[rows, :], k, me.other())

    def ys(self):
        me = self.me
        self.c2 = []
        for k in (1, 2, 3):
            landed([self.c1[k]])
            rows = rows_of((me.y + k) % 4, TQ)
            self.t1b[rows, :] = (self.acc[rows, self.mine] + self.r1[rows, :].astype(F32)).astype(BF)
            self.c2.append(self.go(self.t1b.at[rows, :], self.r2.at[k - 1], 3 + k, me.at_y(k)))

    def zs(self):
        me = self.me
        landed([self.c1[0]])
        rows = rows_of(me.y, TQ)
        total = self.acc[rows, self.mine] + self.r1[rows, :].astype(F32)
        landed(self.c2)
        for k in range(3):
            total = total + self.r2[k].astype(F32)
        self.t2b[...] = total.astype(BF)
        for q in range(NRED):

            @pl.when(me.z != q)
            def _():
                remote(
                    self.t2b.at[q * RQ : (q + 1) * RQ, :],
                    self.r3.at[me.z],
                    self.sems.at[0, 7 + q],
                    self.sems.at[1, 7 + me.z],
                    me.dev(z=q),
                ).start()

    def reduce(self, final, post):
        me = self.me
        self.final = final

        @pl.when(me.z < NRED)
        def _():
            self.r3[me.z] = self.t2b[rows_of(me.z, RQ), :]
            for s in range(8):

                @pl.when(me.z != s)
                def _():
                    remote(
                        self.t2b.at[0:RQ, :],
                        self.r3.at[s],
                        self.sems.at[0, 7],
                        self.sems.at[1, 7 + s],
                        me.other(),
                    ).wait_recv()

            rows = pl.ds(pl.multiple_of(me.y * TQ + me.z * RQ, RQ), RQ)
            total = self.r3[0].astype(F32)
            for s in range(1, 8):
                total = total + self.r3[s].astype(F32)
            final[rows, self.mine] = post(total, rows, self.mine)
            for k in range(1, 8):
                piece = final.at[rows, self.mine]
                remote(
                    piece, piece, self.sems.at[0, 14 + k], self.sems.at[1, 15 + me.z], me.at_z(k)
                ).start()

    def spread(self):
        me, final = self.me, self.final
        for q in range(NRED):
            piece = final.at[pl.ds(pl.multiple_of(me.y * TQ + q * RQ, RQ), RQ), self.mine]

            @pl.when(me.z != q)
            def _():
                remote(piece, piece, self.sems.at[0, 7], self.sems.at[1, 15 + q], me.other()).wait_recv()

        rows = rows_of(me.y, TQ)
        block = final.at[rows, self.mine]
        self.c5 = [self.go(block, block, 21 + k, me.at_y(k)) for k in (1, 2, 3)]
        block = final.at[rows, self.back]
        self.c6 = [self.go(block, block, 25, me.other())]

    def collect(self):
        me, final = self.me, self.final
        for k in (1, 2, 3):
            landed([self.c5[k - 1]])
            block = final.at[rows_of((me.y + 4 - k) % 4, TQ), self.back]
            self.c6.append(self.go(block, block, 25 + k, me.other()))
        landed(self.c6)

    def drain(self):
        me = self.me
        for q in range(NRED):

            @pl.when(me.z != q)
            def _():
                remote(
                    self.t2b.at[q * RQ : (q + 1) * RQ, :],
                    self.r3.at[me.z],
                    self.sems.at[0, 7 + q],
                    self.sems.at[1, 7 + me.z],
                    me.dev(z=q),
                ).wait_send()

        @pl.when(me.z < NRED)
        def _():
            for k in range(1, 8):
                remote(
                    self.t2b.at[0:RQ, :],
                    self.t2b.at[0:RQ, :],
                    self.sems.at[0, 14 + k],
                    self.sems.at[1, 15],
                    me.other(),
                ).wait_send()


def chunk_scratch(width):
    return [
        pltpu.VMEM((TOK, width), BF),
        pltpu.VMEM((TOK, width), BF),
        pltpu.VMEM((3, TQ, width), BF),
        pltpu.VMEM((TQ, width), BF),
        pltpu.VMEM((8, RQ, width), BF),
        pltpu.SemaphoreType.DMA((2, 30)),
    ]


class ScalarSum:
    def __init__(self, me, fl, buf, sems):
        self.me, self.fl, self.buf, self.sems = me, fl, buf, sems

    def go(self, stage, tile):
        me = self.me
        index, base, count, at = (
            (me.x, 0, 4, me.at_x),
            (me.f, 4, 16, me.at_f),
            (me.t, 20, 4, me.at_t),
        )[stage]
        mine = self.buf.at[base + index]
        self.buf[base + index] = tile
        self.copies = []
        for k in range(1, count):
            self.copies.append(
                self.fl.start(mine, mine, self.sems.at[0, base + k], self.sems.at[1, base + k], at(k))
            )
        self.span = (base, count)

    def get(self):
        landed(self.copies)
        base, count = self.span
        total = self.buf[base]
        for s in range(1, count):
            total = total + self.buf[base + s]
        return total


def whole_sum(value):
    return jnp.sum(jnp.sum(value, axis=1, keepdims=True), axis=0, keepdims=True)


def fold(value):
    return jnp.sum(value.reshape(BLK // 8, 8, DB), axis=0)


def tile_of(values):
    rows = [jnp.broadcast_to(v, (1, 128)) for v in values]
    while len(rows) < 8:
        rows.append(jnp.zeros((1, 128), F32))
    return jnp.concatenate(rows, axis=0)


def add_x(send, slots, rows, i):
    total = send[i, rows, :].astype(F32)
    for k in range(3):
        total = total + slots[k, i].astype(F32)
    return total


def whole_low(c):
    return c * 512


def whole_back(c):
    return c * 640


def outer_low(c):
    return c * 768


def inner_low(c):
    return 384 + c * 128


def inner_back(c):
    return 384 + c * 256


def kernel(
    x, target, in_wg, in_wu, in_wd, in_sg, in_su, in_sd,
    out_g, out_u, out_d, hess, ray,
    out_w, near_r, full_r, far_r, sems_w, sems_n, sems_l, sems_p,
    parts, w_down, s_down, start_t, one, cross_s, cross_r,
    kp, kr, kpair, sems_k,
    send_a, slots_a, sems_a, send_d, slots_d, sems_d,
    own, hh, sems_h, mm, sems_m,
    acc_o, send_o, acc_p, send_p,
    o0, o1, o2, o3, o4, o5, p0, p1, p2, p3, p4, p5,
    go, gd,
    send_b, slots_b, sems_b, send_c, slots_c, sems_c,
    gu1, sems_g1, u1d, tan2, h2,
    q0, q1, q2, q3, q4, q5, r0, r1, r2, r3, r4, r5,
    g2,
    send_f, slots_f, sems_f,
    gu2, sems_g2,
    sbuf1, ssem1, sbuf2, ssem2,
):
    me = Place()
    fl = Flight()
    twos = (out_g, out_u, out_d)

    barrier = pltpu.get_barrier_semaphore()
    peers = (
        [me.at_f(k) for k in range(1, NF)]
        + [me.at_t(k) for k in (1, 2, 3)]
        + [me.at_x(k) for k in (1, 2, 3)]
        + [me.across(low) for low in range(4)]
    )
    for peer in peers:
        pl.semaphore_signal(barrier, inc=1, device_id=peer, device_id_type=MESH)

    pairs = ((in_wg, in_wu), (in_sg, in_su), (in_wd, in_sd))
    flights = []

    with jax.named_scope("regroup"):
        pack(*pairs[0], out_w.at[0])
        pl.semaphore_wait(barrier, len(peers))
        flights.append(send_near(me, fl, out_w.at[0], near_r.at[0], sems_n.at[0], sems_l.at[0]))
        pack(*pairs[1], out_w.at[1])
        flights.append(send_near(me, fl, out_w.at[1], near_r.at[1], sems_n.at[1], sems_l.at[1]))
        pack(*pairs[2], out_w.at[2])
        parts[...] = jnp.zeros(parts.shape, BF)

    def squares(b, total):
        rows = pl.ds(pl.multiple_of(b * 8, 8), 8)
        for ref in (in_sg, in_su, in_sd):
            v = ref[rows, :].astype(F32) * SCALE
            total = total + v * v
        return total

    with jax.named_scope("gram"):
        kp[...] = nt(x[...], x[...])
        c_k = []
        for k in (1, 2, 3):
            c_k.append(fl.start(kp, kr.at[k - 1], sems_k.at[0, k - 1], sems_k.at[1, k - 1], me.at_x(k)))
        start_square = lax.fori_loop(0, WR // 8, squares, jnp.zeros((8, FF // 4), F32))
        start_square = whole_sum(start_square)

    def partial(send, i, value):
        send[i] = value.astype(BF)

    my_rows = rows_of(me.x, TQ)

    def products(p, send):
        for q in range(2):
            unpack_half(me.half, near_r.at[p, q], parts.at[q, 2 * p], parts.at[q, 2 * p + 1])
            for i in range(2):
                partial(send, 2 * q + i, nn(x[...], parts[q, 2 * p + i]))

    def cross(p, send, slots):
        for i in range(2):
            cross_s[p, i] = add_x(send, slots, my_rows, 2 + i).astype(BF)
        return fl.start(cross_s.at[p], cross_r.at[p], sems_p.at[0, p], sems_p.at[1, p], me.partner())

    def joined(p, send, slots, i):
        return add_x(send, slots, my_rows, i) + cross_r[p, i].astype(F32)

    with jax.named_scope("forward"):
        blocks_landed(flights[0])
        flights.append(send_blocks(me, fl, out_w.at[2], full_r, sems_w, sems_l.at[2, 0]))
        products(0, send_a)
        c_a = scatter_x(me, fl, send_a, slots_a, sems_a)
        blocks_landed(flights[1])
        products(1, send_d)
        landed(c_a)
        cross_a = cross(0, send_a, slots_a)
        c_d = scatter_x(me, fl, send_d, slots_d, sems_d)
    with jax.named_scope("hidden"):
        landed([cross_a])
        gate_pre, up_pre = joined(0, send_a, slots_a, 0), joined(0, send_a, slots_a, 1)
        val, slope, curve = gelu_parts(gate_pre)
        slope_up = slope * up_pre
        hh[0, my_rows, :] = (val * up_pre).astype(BF)
        c_h0 = gather_x(me, fl, hh.at[0:1], sems_h.at[0])
        mm[0, my_rows, :] = slope_up
        mm[1, my_rows, :] = val
        own[0] = slope
        own[1] = up_pre * curve
        landed(c_d)
        cross_d = cross(1, send_d, slots_d)

    def transposed(i, s):
        for b in range(DB // 128):
            cols = slice(b * 128, (b + 1) * 128)
            start_t[i, :, cols] = s[cols, :].astype(F32).T.astype(BF)

    with jax.named_scope("starts"):
        blocks_landed(flights[2])
        for i in range(NF // 2):
            rows = slice(i * 2 * WR, (i + 1) * 2 * WR)
            unpack(full_r.at[2 * i], full_r.at[2 * i + 1], w_down, s_down, rows)

    def far(part):
        blocks = pl.ds(part * 4, 4)
        return fl.start(
            near_r.at[1, 1, blocks], far_r.at[blocks], sems_p.at[0, 2 + part], sems_p.at[1, 2 + part], me.partner()
        )

    def out_post(total, rows, lanes):
        return ((total - target[rows, lanes].astype(F32)) / float(TOK)).astype(BF)

    def dot_post(total, rows, lanes):
        return (total / float(TOK)).astype(BF)

    ch_o = Chunk(me, fl, acc_o, send_o, (o0, o1, o2, o3, o4, o5), whole_low, 640, whole_back, 512)
    ch_p = Chunk(me, fl, acc_p, send_p, (p0, p1, p2, p3, p4, p5), whole_low, 640, whole_back, 512)
    with jax.named_scope("outputs"):
        landed(c_h0)
        ch_o.put(nt(hh[0], w_down[...]))
        ch_o.cores()
        landed([cross_d])
        gate_dot, up_dot = joined(1, send_d, slots_d, 0), joined(1, send_d, slots_d, 1)
        hh[1, my_rows, :] = (mm[0, my_rows, :] * gate_dot + mm[1, my_rows, :] * up_dot).astype(BF)
        c_h1 = gather_x(me, fl, hh.at[1:2], sems_h.at[1])
        own[2] = gate_dot
        own[3] = up_dot
        ch_o.ys()
        landed(c_h1)
        c_m = gather_x(me, fl, mm, sems_m)
        ch_p.put(nt(hh[1], w_down[...]) + nt(hh[0], s_down[...]))
        ch_p.cores()
        ch_o.zs()
        ch_p.ys()
        ch_o.reduce(go, out_post)
        ch_p.zs()
        ch_o.spread()
        ch_p.reduce(gd, dot_post)
        ch_o.collect()
    with jax.named_scope("back"):
        partial(send_b, 0, nn(go[...], w_down[...]))
        c_b = scatter_x(me, fl, send_b, slots_b, sems_b)
        c_far = [far(0)]
        ch_p.spread()
        ch_p.collect()
        partial(send_c, 0, nn(gd[...], w_down[...]) + nn(go[...], s_down[...]))
        c_c = scatter_x(me, fl, send_c, slots_c, sems_c)
        image = tn(hh[1], go[...]) + tn(hh[0], gd[...])
        one[2] = image
        u1d[...] = image.astype(BF)
        transposed(2, s_down)
        landed(c_b)
        grad_hidden = add_x(send_b, slots_b, my_rows, 0)
        own[0] = grad_hidden * own[0]
        own[1] = grad_hidden * own[1]
        landed(c_c)
        back_dot = add_x(send_c, slots_c, my_rows, 0)
        slope_term, curve_term = own[0], own[1]
        gu1[0, my_rows, :] = (
            back_dot * mm[0, my_rows, :] + slope_term * own[3] + curve_term * own[2]
        ).astype(BF)
        gu1[1, my_rows, :] = (back_dot * mm[1, my_rows, :] + slope_term * own[2]).astype(BF)
        c_g1 = gather_x(me, fl, gu1, sems_g1)
        landed(c_m)
        landed(c_k)
        total = kp[...] + (kr[0] + kr[1] + kr[2])
        high = total.astype(BF)
        kpair[0] = high
        kpair[1] = (total - high.astype(F32)).astype(BF)
        landed(c_g1)

    with jax.named_scope("second"):
        for i in range(2):
            tan2[i] = nn(kpair[0], gu1[i]) + nn(kpair[1], gu1[i])
        h2[...] = (mm[0] * tan2[0] + mm[1] * tan2[1]).astype(BF)
        ch_q = Chunk(me, fl, acc_o, send_o, (q0, q1, q2, q3, q4, q5), outer_low, 384, outer_low, 384)
        ch_r = Chunk(me, fl, acc_o, send_o, (r0, r1, r2, r3, r4, r5), inner_low, 256, inner_back, 128)
        for copy in ch_o.c1.values():
            copy.wait_send()
        done = [id(copy) for copy in ch_o.c1.values()]
        fl.sent = [copy for copy in fl.sent if id(copy) not in done]
        ch_q.put(nt(h2[...], w_down[...]) + nn(hh[0], u1d[...]))
        ch_q.cores()
        ch_r.cores()
        ch_q.ys()
        ch_r.ys()

    def dots_one(b, carry):
        rows = rows_of(b, BLK)
        su, uu = carry
        s = start_t[2, rows, :].astype(F32) * SCALE
        u = one[2, rows, :] * SCALE
        return su + fold(s * u), uu + fold(u * u)

    zero = jnp.zeros((8, DB), F32)
    sum1 = ScalarSum(me, fl, sbuf1, ssem1)
    with jax.named_scope("image"):
        one[0] = tn(gu1[0], x[...])
        one[1] = tn(gu1[1], x[...])
        ch_q.zs()
        ch_r.zs()
        su, uu = lax.fori_loop(0, HB // BLK, dots_one, (zero, zero))
        su, uu = whole_sum(su), whole_sum(uu)
        for i in range(2):
            g = gu1[i, my_rows, :].astype(F32) * SCALE
            su = su + whole_sum(own[2 + i] * SCALE * g)
            uu = uu + whole_sum(tan2[i, my_rows, :] * SCALE * g)
        ch_q.reduce(g2, dot_post)
        ch_r.reduce(g2, dot_post)
        sum1.go(0, tile_of([start_square, su, uu]))
        ch_q.spread()
        ch_r.spread()
        sum1.go(1, sum1.get())
        ch_q.collect()
        ch_r.collect()

    with jax.named_scope("back_second"):
        partial(send_f, 0, nn(g2[...], w_down[...]) + nt(go[...], u1d[...]))
        c_f = scatter_x(me, fl, send_f, slots_f, sems_f)
        c_far.append(far(1))
        out_d[...] = tn(h2[...], go[...]) + tn(hh[0], g2[...])
        sum1.go(2, sum1.get())
        landed(c_f)
        back_dot = add_x(send_f, slots_f, my_rows, 0)
        gate_two = tan2[0, my_rows, :]
        up_two = tan2[1, my_rows, :]
        gu2[0, my_rows, :] = (
            back_dot * mm[0, my_rows, :] + own[0] * up_two + own[1] * gate_two
        ).astype(BF)
        gu2[1, my_rows, :] = (back_dot * mm[1, my_rows, :] + own[0] * gate_two).astype(BF)
        c_g2 = gather_x(me, fl, gu2, sems_g2)
        norms = sum1.get() * (1.0 / (SCALE * SCALE * ENTRIES))
    s_s, s_u, u_u = norms[0:1, 0:1], norms[1:2, 0:1], norms[2:3, 0:1]
    f = 1.0 / jnp.sqrt(s_s + EPS)
    v11 = f * f * s_s
    h11 = f * f * s_u
    w11 = f * f * u_u
    rr = jnp.maximum(w11 - h11 * h11 * (2.0 - v11), 0.0)
    h21 = jnp.sqrt(rr + EPS)
    v12 = (h11 - h11 * v11) / h21
    v22 = rr / (h21 * h21)
    a1 = f / h21
    a0 = -h11 * f / h21

    def dots_two(b, carry):
        rows = rows_of(b, BLK)
        p1, p2, pw = carry
        s = start_t[2, rows, :].astype(F32)
        u = one[2, rows, :]
        w = (a1 * out_d[rows, :] + a0 * u) * SCALE
        first = f * s * SCALE
        second = (a1 * u + a0 * s) * SCALE
        return p1 + fold(first * w), p2 + fold(second * w), pw + fold(w * w)

    with jax.named_scope("last_dots"):
        d1, d2, dw = lax.fori_loop(0, HB // BLK, dots_two, (zero, zero, zero))
        d1, d2, dw = whole_sum(d1), whole_sum(d2), whole_sum(dw)
        for i in range(2):
            w = (
                a1 * gu2[i, my_rows, :].astype(F32) + a0 * gu1[i, my_rows, :].astype(F32)
            ) * SCALE
            first = own[2 + i]
            second = a1 * tan2[i, my_rows, :] + a0 * first
            d1 = d1 + whole_sum((f * SCALE) * first * w)
            d2 = d2 + whole_sum(second * SCALE * w)
        sum2 = ScalarSum(me, fl, sbuf2, ssem2)
        sum2.go(0, tile_of([d1, d2, dw]))
        landed(c_g2)
        dw = jnp.zeros((1, 1), F32)
        for i in range(2):
            w = (a1 * gu2[i].astype(F32) + a0 * gu1[i].astype(F32)) * SCALE
            high = w.astype(BF)
            low = (w - high.astype(F32)).astype(BF)
            kw = nn(kpair[0], high) + nn(kpair[1], high) + nn(kpair[0], low)
            dw = dw + whole_sum(w * kw)
        blank = jnp.zeros((1, 1), F32)
        sum2.go(1, sum2.get() + tile_of([blank, blank, dw]))
        out_g[...] = tn(gu2[0], x[...])
        sum2.go(2, sum2.get())
        out_u[...] = tn(gu2[1], x[...])
        landed(c_far)
        unpack_half(1 - me.half, far_r, parts.at[0, 2], parts.at[0, 3])
        transposed(0, parts.at[0, 2])
        transposed(1, parts.at[0, 3])
        norms = sum2.get() * (1.0 / (SCALE * SCALE * ENTRIES))
    h12, h22, ww = norms[0:1, 0:1], norms[1:2, 0:1], norms[2:3, 0:1]
    rr = (
        ww
        - 2.0 * (h12 * h12 + h22 * h22)
        + h12 * h12 * v11
        + h22 * h22 * v22
        + 2.0 * h12 * h22 * v12
    )
    h32 = jnp.sqrt(jnp.maximum(rr, 0.0) + EPS)
    c2 = a1 / h32
    c1 = (a0 - h22 * a1) / h32
    c0 = -(h12 * f + h22 * a0) / h32
    for i, value in enumerate((h21, h12, h22, h32)):
        hess[i] = jnp.max(value)
    ray[0] = jnp.max(h11)

    def third(b, carry):
        rows = rows_of(b, BLK)
        for i in range(3):
            twos[i][rows, :] = (
                c2 * twos[i][rows, :] + c1 * one[i, rows, :] + c0 * start_t[i, rows, :].astype(F32)
            )
        return carry

    with jax.named_scope("third"):
        lax.fori_loop(0, HB // BLK, third, 0)

    for copy in fl.sent:
        copy.wait_send()
    for chunk in (ch_o, ch_p, ch_q, ch_r):
        chunk.drain()


def rounds(*operands):
    dma = pltpu.SemaphoreType.DMA

    def xround(n):
        return [pltpu.VMEM((n, TOK, HB), BF), pltpu.VMEM((3, n, TQ, HB), BF), dma((2, 3))]

    scratch = (
        [pltpu.VMEM((3, NF, BR, WL), BF), pltpu.VMEM((2, 2, 8, BR, WL), BF), pltpu.VMEM((NF, BR, WL), BF), pltpu.VMEM((8, BR, WL), BF)]
        + [dma((2, NF)), dma((2, 2, 2, 8)), dma((3, 2)), dma((2, 4))]
        + [pltpu.VMEM((2, 4, DB, HB), BF)] + [pltpu.VMEM((DB, HB), BF)] * 2
        + [pltpu.VMEM((3, HB, DB), BF), pltpu.VMEM((3, HB, DB), F32)] + [pltpu.VMEM((2, 2, TQ, HB), BF)] * 2
        + [pltpu.VMEM((TOK, TOK), F32), pltpu.VMEM((3, TOK, TOK), F32), pltpu.VMEM((2, TOK, TOK), BF), dma((2, 3))]
        + xround(4) + xround(4)
        + [pltpu.VMEM((4, TQ, HB), F32), pltpu.VMEM((2, TOK, HB), BF), dma((2, 2, 3)), pltpu.VMEM((2, TOK, HB), F32), dma((2, 3))]
        + [pltpu.VMEM((TOK, DB), F32), pltpu.VMEM((TOK, DB), BF)] * 2
        + chunk_scratch(640) + chunk_scratch(640)
        + [pltpu.VMEM((TOK, DB), BF)] * 2
        + xround(1) + xround(1)
        + [pltpu.VMEM((2, TOK, HB), BF), dma((2, 3)), pltpu.VMEM((HB, DB), BF), pltpu.VMEM((2, TOK, HB), F32), pltpu.VMEM((TOK, HB), BF)]
        + chunk_scratch(384) + chunk_scratch(256)
        + [pltpu.VMEM((TOK, DB), BF)]
        + xround(1)
        + [pltpu.VMEM((2, TOK, HB), BF), dma((2, 3))]
        + [pltpu.VMEM((24, 8, 128), F32), dma((2, 24)), pltpu.VMEM((24, 8, 128), F32), dma((2, 24))]
    )
    wide = jax.ShapeDtypeStruct((HB, DB), F32)
    return pl.pallas_call(
        kernel,
        out_shape=(wide, wide, wide, jax.ShapeDtypeStruct((4,), F32), jax.ShapeDtypeStruct((1,), F32)),
        in_specs=[pl.BlockSpec(memory_space=pltpu.VMEM)] * 8,
        out_specs=[pl.BlockSpec(memory_space=pltpu.VMEM)] * 3 + [pl.BlockSpec(memory_space=pltpu.SMEM)] * 2,
        scratch_shapes=scratch,
        compiler_params=pltpu.CompilerParams(
            collective_id=0, has_side_effects=True, vmem_limit_bytes=60 * 1024 * 1024
        ),
        name="arnoldi",
    )(*operands)


def on_device(inputs, target, w_gate, w_up, w_down, start_gate, start_up, start_down):
    third_g, third_u, third_d, hess, ray = rounds(
        inputs, target, w_gate, w_up, w_down.T, start_gate, start_up, start_down.T
    )
    return (
        third_g.T.reshape(DB, 1, HB),
        third_u.T.reshape(DB, 1, HB),
        third_d.reshape(1, HB, DB),
        hess,
        ray,
    )


def solution(mesh):
    placed = (
        P(None, "dcn"),
        P(None, "dcn"),
        P(("dcn", "fsdp"), "tp"),
        P(("dcn", "fsdp"), "tp"),
        P("tp", ("dcn", "fsdp")),
        P(("dcn", "fsdp"), "tp"),
        P(("dcn", "fsdp"), "tp"),
        P("tp", ("dcn", "fsdp")),
    )
    return jax.shard_map(
        on_device,
        mesh=mesh,
        in_specs=placed,
        out_specs=(
            P("dcn", "tp", "fsdp"),
            P("dcn", "tp", "fsdp"),
            P("tp", "fsdp", "dcn"),
            P(),
            P(),
        ),
        check_vma=False,
    )
```

```python
import math

import jax
import jax.numpy as jnp
from jax import lax
from jax.experimental import pallas as pl
from jax.experimental.pallas import tpu as pltpu
from jax.sharding import PartitionSpec as P

D = 4608
FF = 18432
TOK = 320
DB = 1152
HB = 288
TQ = 80
RQ = 16
NRED = 5
BLK = 48
NF = 16
WR = 72
WL = 256
SR = 24
BR = 176
ENTRIES = float(3 * D * FF)
EPS = 1e-06
SCALE = 2.0**-14
MESH = pl.DeviceIdType.MESH
BF = jnp.bfloat16
F32 = jnp.float32

gelu_cubic = 0.044715
gelu_scale = math.sqrt(2.0 / math.pi)


def gelu_parts(argument):
    squared = argument * argument
    inner_arg = gelu_scale * (argument + gelu_cubic * squared * argument)
    tanh_val = jnp.tanh(inner_arg)
    sech_square = 1.0 - tanh_val * tanh_val
    inner_slope = gelu_scale * (1.0 + 3.0 * gelu_cubic * squared)
    inner_curve = gelu_scale * 6.0 * gelu_cubic * argument
    gelu_val = 0.5 * argument * (1.0 + tanh_val)
    gelu_slope = 0.5 * (1.0 + tanh_val) + 0.5 * argument * sech_square * inner_slope
    gelu_curve = sech_square * inner_slope + 0.5 * argument * (
        sech_square * inner_curve - 2.0 * tanh_val * sech_square * inner_slope * inner_slope
    )
    return (gelu_val, gelu_slope, gelu_curve)


def nn(a, b):
    return lax.dot_general(a, b, (((1,), (0,)), ((), ())), preferred_element_type=F32)


def nt(a, b):
    return lax.dot_general(a, b, (((1,), (1,)), ((), ())), preferred_element_type=F32)


def tn(a, b):
    return lax.dot_general(a, b, (((0,), (0,)), ((), ())), preferred_element_type=F32)


class Place:
    def __init__(self):
        self.x = lax.axis_index("dcn")
        fsdp = lax.axis_index("fsdp")
        tp = lax.axis_index("tp")
        self.f = fsdp
        self.t = tp
        self.y = fsdp // 4
        self.half = (fsdp % 4) // 2
        self.m = self.y * 2 + fsdp % 2
        self.p = fsdp + 2 - 4 * self.half
        self.z = (tp // 2) * 4 + fsdp % 4
        self.c = tp % 2

    def dev(self, x=None, y=None, z=None, c=None):
        x = self.x if x is None else x
        y = self.y if y is None else y
        z = self.z if z is None else z
        c = self.c if c is None else c
        return (x, y * 4 + z % 4, (z // 4) * 2 + c)

    def at_x(self, k):
        return self.dev(x=(self.x + k) % 4)

    def at_y(self, k):
        return self.dev(y=(self.y + k) % 4)

    def at_z(self, k):
        return self.dev(z=(self.z + k) % 8)

    def at_f(self, k):
        return (self.x, (self.f + k) % NF, self.t)

    def near(self, k):
        m = (self.m + k) % 8
        f = (m // 2) * 4 + self.half * 2 + m % 2
        return f, f + 2 - 4 * self.half

    def partner(self):
        return (self.x, self.p, self.t)

    def at_t(self, k):
        return (self.x, self.f, (self.t + k) % 4)

    def across(self, low):
        return self.dev(z=(1 - self.z // 4) * 4 + low)

    def other(self):
        return self.dev(c=1 - self.c)


def rows_of(index, size):
    return pl.ds(pl.multiple_of(index * size, size), size)


def lanes_at(start, size):
    return pl.ds(pl.multiple_of(start, 128), size)


def remote(src, dst, ssem, rsem, dev):
    return pltpu.make_async_remote_copy(
        src_ref=src, dst_ref=dst, send_sem=ssem, recv_sem=rsem, device_id=dev, device_id_type=MESH
    )


class Flight:
    def __init__(self):
        self.sent = []

    def start(self, src, dst, ssem, rsem, dev):
        copy = remote(src, dst, ssem, rsem, dev)
        copy.start()
        self.sent.append(copy)
        return copy


def pack(first, second, out):
    lane = lax.broadcasted_iota(jnp.int32, (SR, 128), 1)
    for j in range(NF):
        lanes = slice(j * HB, j * HB + WL)
        wide = jnp.concatenate([first[:, lanes].astype(F32), second[:, lanes].astype(F32)], axis=0)
        start = j * HB + WL
        base = start - start % 128
        both = jnp.concatenate(
            [first[:, base : base + 128].astype(F32), second[:, base : base + 128].astype(F32)], axis=0
        )
        tiles = []
        for group in ((0, 1, 2, 3), (4, 5)):
            tile = jnp.zeros((SR, 128), F32)
            for g in group:
                strip = both[g * SR : (g + 1) * SR]
                at = (32 * g) % 128
                shift = (at - start) % 128
                if shift:
                    strip = pltpu.roll(strip, shift, axis=1)
                tile = jnp.where((lane >= at) & (lane < at + 32), strip, tile)
            tiles.append(tile)
        rest = jnp.concatenate(tiles, axis=1)
        blank = jnp.zeros((BR - 2 * WR - SR, WL), F32)
        out[j] = jnp.concatenate([wide, rest, blank], axis=0).astype(BF)


def unpack(a, b, first, second, rows):
    a, b = a[...].astype(F32), b[...].astype(F32)
    rests = []
    for v in (a, b):
        strips = []
        for g in range(6):
            at = 32 * g
            tile = v[2 * WR : 2 * WR + SR, at - at % 128 : at - at % 128 + 128]
            if at % 128:
                tile = pltpu.roll(tile, 128 - at % 128, axis=1)
            strips.append(tile)
        rests.append(jnp.concatenate(strips, axis=0))
    first[rows, 0:WL] = jnp.concatenate([a[:WR], b[:WR]], axis=0).astype(BF)
    second[rows, 0:WL] = jnp.concatenate([a[WR : 2 * WR], b[WR : 2 * WR]], axis=0).astype(BF)
    a, b = rests
    first[rows, WL:HB] = jnp.concatenate([a[:WR], b[:WR]], axis=0)[:, 0:32].astype(BF)
    second[rows, WL:HB] = jnp.concatenate([a[WR:], b[WR:]], axis=0)[:, 0:32].astype(BF)


def unpack_half(half, blocks, first, second):
    for y in range(4):
        rows = pl.ds(pl.multiple_of(y * 4 * WR + half * 2 * WR, 2 * WR), 2 * WR)
        unpack(blocks.at[2 * y], blocks.at[2 * y + 1], first, second, rows)


def send_blocks(me, fl, out, land, sems, lsem):
    copies = []
    for k in range(1, NF):
        copies.append(
            fl.start(out.at[(me.f + k) % NF], land.at[me.f], sems.at[0, k], sems.at[1, k], me.at_f(k))
        )
    own = pltpu.make_async_copy(out.at[me.f], land.at[me.f], lsem)
    own.start()
    return copies, (own,)


def send_near(me, fl, out, land, sems, lsems):
    copies = []
    for k in range(1, 8):
        f, p = me.near(k)
        for q, j in enumerate((f, p)):
            copies.append(
                fl.start(
                    out.at[j], land.at[q, me.m], sems.at[0, q, k], sems.at[1, q, k], (me.x, f, me.t)
                )
            )
    own = []
    for q, j in enumerate((me.f, me.p)):
        own.append(pltpu.make_async_copy(out.at[j], land.at[q, me.m], lsems.at[q]))
        own[-1].start()
    return copies, own


def blocks_landed(flight):
    landed(flight[0])
    for copy in flight[1]:
        copy.wait()


def scatter_x(me, fl, stage, slots, sems):
    out = []
    for k in (1, 2, 3):
        peer = (me.x + k) % 4
        out.append(
            fl.start(
                stage.at[:, rows_of(peer, TQ), :],
                slots.at[k - 1],
                sems.at[0, k - 1],
                sems.at[1, k - 1],
                me.at_x(k),
            )
        )
    return out


def gather_x(me, fl, buf, sems):
    out = []
    mine = buf.at[:, rows_of(me.x, TQ), :]
    for k in (1, 2, 3):
        out.append(fl.start(mine, mine, sems.at[0, k - 1], sems.at[1, k - 1], me.at_x(k)))
    return out


def landed(copies):
    for copy in copies:
        copy.wait_recv()


class Chunk:
    def __init__(self, me, fl, acc, send, scratch, low, width, back, back_width):
        self.me, self.fl, self.acc, self.send = me, fl, acc, send
        (self.r1, self.t1b, self.r2, self.t2b, self.r3, self.sems) = scratch
        self.mine = lanes_at(low(me.c), width)
        self.theirs = lanes_at(low(1 - me.c), width)
        self.back = lanes_at(back(me.c), back_width)

    def go(self, src, dst, sem, dev, rsem=None):
        return self.fl.start(src, dst, self.sems.at[0, sem], self.sems.at[1, sem], dev)

    def put(self, value):
        self.acc[...] = value
        self.send[...] = value.astype(BF)

    def cores(self):
        me = self.me
        self.c1 = {}
        for k in (1, 2, 3, 0):
            rows = rows_of((me.y + k) % 4, TQ)
            self.c1[k] = self.go(self.send.at[rows, self.theirs], self.r1.at[rows, :], k, me.other())

    def ys(self):
        me = self.me
        self.c2 = []
        for k in (1, 2, 3):
            landed([self.c1[k]])
            rows = rows_of((me.y + k) % 4, TQ)
            self.t1b[rows, :] = (self.acc[rows, self.mine] + self.r1[rows, :].astype(F32)).astype(BF)
            self.c2.append(self.go(self.t1b.at[rows, :], self.r2.at[k - 1], 3 + k, me.at_y(k)))

    def zs(self):
        me = self.me
        landed([self.c1[0]])
        rows = rows_of(me.y, TQ)
        total = self.acc[rows, self.mine] + self.r1[rows, :].astype(F32)
        landed(self.c2)
        for k in range(3):
            total = total + self.r2[k].astype(F32)
        self.t2b[...] = total.astype(BF)
        for q in range(NRED):

            @pl.when(me.z != q)
            def _():
                remote(
                    self.t2b.at[q * RQ : (q + 1) * RQ, :],
                    self.r3.at[me.z],
                    self.sems.at[0, 7 + q],
                    self.sems.at[1, 7 + me.z],
                    me.dev(z=q),
                ).start()

    def reduce(self, final, post):
        me = self.me
        self.final = final

        @pl.when(me.z < NRED)
        def _():
            self.r3[me.z] = self.t2b[rows_of(me.z, RQ), :]
            for s in range(8):

                @pl.when(me.z != s)
                def _():
                    remote(
                        self.t2b.at[0:RQ, :],
                        self.r3.at[s],
                        self.sems.at[0, 7],
                        self.sems.at[1, 7 + s],
                        me.other(),
                    ).wait_recv()

            rows = pl.ds(pl.multiple_of(me.y * TQ + me.z * RQ, RQ), RQ)
            total = self.r3[0].astype(F32)
            for s in range(1, 8):
                total = total + self.r3[s].astype(F32)
            final[rows, self.mine] = post(total, rows, self.mine)
            for k in range(1, 8):
                piece = final.at[rows, self.mine]
                remote(
                    piece, piece, self.sems.at[0, 14 + k], self.sems.at[1, 15 + me.z], me.at_z(k)
                ).start()

    def spread(self):
        me, final = self.me, self.final
        for q in range(NRED):
            piece = final.at[pl.ds(pl.multiple_of(me.y * TQ + q * RQ, RQ), RQ), self.mine]

            @pl.when(me.z != q)
            def _():
                remote(piece, piece, self.sems.at[0, 7], self.sems.at[1, 15 + q], me.other()).wait_recv()

        rows = rows_of(me.y, TQ)
        block = final.at[rows, self.mine]
        self.c5 = [self.go(block, block, 21 + k, me.at_y(k)) for k in (1, 2, 3)]
        block = final.at[rows, self.back]
        self.c6 = [self.go(block, block, 25, me.other())]

    def collect(self):
        me, final = self.me, self.final
        for k in (1, 2, 3):
            landed([self.c5[k - 1]])
            block = final.at[rows_of((me.y + 4 - k) % 4, TQ), self.back]
            self.c6.append(self.go(block, block, 25 + k, me.other()))
        landed(self.c6)

    def drain(self):
        me = self.me
        for q in range(NRED):

            @pl.when(me.z != q)
            def _():
                remote(
                    self.t2b.at[q * RQ : (q + 1) * RQ, :],
                    self.r3.at[me.z],
                    self.sems.at[0, 7 + q],
                    self.sems.at[1, 7 + me.z],
                    me.dev(z=q),
                ).wait_send()

        @pl.when(me.z < NRED)
        def _():
            for k in range(1, 8):
                remote(
                    self.t2b.at[0:RQ, :],
                    self.t2b.at[0:RQ, :],
                    self.sems.at[0, 14 + k],
                    self.sems.at[1, 15],
                    me.other(),
                ).wait_send()


def chunk_scratch(width):
    return [
        pltpu.VMEM((TOK, width), BF),
        pltpu.VMEM((TOK, width), BF),
        pltpu.VMEM((3, TQ, width), BF),
        pltpu.VMEM((TQ, width), BF),
        pltpu.VMEM((8, RQ, width), BF),
        pltpu.SemaphoreType.DMA((2, 30)),
    ]


class ScalarSum:
    def __init__(self, me, fl, buf, sems):
        self.me, self.fl, self.buf, self.sems = me, fl, buf, sems

    def go(self, stage, tile):
        me = self.me
        index, base, count, at = (
            (me.x, 0, 4, me.at_x),
            (me.f, 4, 16, me.at_f),
            (me.t, 20, 4, me.at_t),
        )[stage]
        mine = self.buf.at[base + index]
        self.buf[base + index] = tile
        self.copies = []
        for k in range(1, count):
            self.copies.append(
                self.fl.start(mine, mine, self.sems.at[0, base + k], self.sems.at[1, base + k], at(k))
            )
        self.span = (base, count)

    def get(self):
        landed(self.copies)
        base, count = self.span
        total = self.buf[base]
        for s in range(1, count):
            total = total + self.buf[base + s]
        return total


def whole_sum(value):
    return jnp.sum(jnp.sum(value, axis=1, keepdims=True), axis=0, keepdims=True)


def fold(value):
    return jnp.sum(value.reshape(BLK // 8, 8, DB), axis=0)


def tile_of(values):
    rows = [jnp.broadcast_to(v, (1, 128)) for v in values]
    while len(rows) < 8:
        rows.append(jnp.zeros((1, 128), F32))
    return jnp.concatenate(rows, axis=0)


def add_x(send, slots, rows, i):
    total = send[i, rows, :].astype(F32)
    for k in range(3):
        total = total + slots[k, i].astype(F32)
    return total


def whole_low(c):
    return c * 512


def whole_back(c):
    return c * 640


def outer_low(c):
    return c * 768


def inner_low(c):
    return 384 + c * 128


def inner_back(c):
    return 384 + c * 256


def kernel(
    x, target, in_wg, in_wu, in_wd, in_sg, in_su, in_sd,
    out_g, out_u, out_d, hess, ray,
    out_w, near_r, full_r, far_r, sems_w, sems_n, sems_l, sems_p,
    parts, w_down, s_down, start_t, one, cross_s, cross_r,
    kp, kr, kpair, sems_k,
    send_a, slots_a, sems_a, send_d, slots_d, sems_d,
    own, hh, sems_h, mm, sems_m,
    acc_o, send_o, acc_p, send_p,
    o0, o1, o2, o3, o4, o5, p0, p1, p2, p3, p4, p5, s0, s1, s2, s3, s4, s5,
    go, gd,
    send_b, slots_b, sems_b, send_c, slots_c, sems_c,
    gu1, sems_g1, u1d, tan2, h2,
    q0, q1, q2, q3, q4, q5, r0, r1, r2, r3, r4, r5,
    g2,
    send_f, slots_f, sems_f,
    gu2, sems_g2,
    sbuf1, ssem1, sbuf2, ssem2,
):
    me = Place()
    fl = Flight()
    twos = (out_g, out_u, out_d)

    barrier = pltpu.get_barrier_semaphore()
    peers = (
        [me.at_f(k) for k in range(1, NF)]
        + [me.at_t(k) for k in (1, 2, 3)]
        + [me.at_x(k) for k in (1, 2, 3)]
        + [me.across(low) for low in range(4)]
    )
    for peer in peers:
        pl.semaphore_signal(barrier, inc=1, device_id=peer, device_id_type=MESH)

    pairs = ((in_wg, in_wu), (in_sg, in_su), (in_wd, in_sd))
    flights = []

    with jax.named_scope("regroup"):
        pack(*pairs[0], out_w.at[0])
        pl.semaphore_wait(barrier, len(peers))
        flights.append(send_near(me, fl, out_w.at[0], near_r.at[0], sems_n.at[0], sems_l.at[0]))
        pack(*pairs[1], out_w.at[1])
        flights.append(send_near(me, fl, out_w.at[1], near_r.at[1], sems_n.at[1], sems_l.at[1]))
        pack(*pairs[2], out_w.at[2])
        parts[...] = jnp.zeros(parts.shape, BF)

    def squares(b, total):
        rows = pl.ds(pl.multiple_of(b * 8, 8), 8)
        for ref in (in_sg, in_su, in_sd):
            v = ref[rows, :].astype(F32) * SCALE
            total = total + v * v
        return total

    with jax.named_scope("gram"):
        kp[...] = nt(x[...], x[...])
        c_k = []
        for k in (1, 2, 3):
            c_k.append(fl.start(kp, kr.at[k - 1], sems_k.at[0, k - 1], sems_k.at[1, k - 1], me.at_x(k)))
        start_square = lax.fori_loop(0, WR // 8, squares, jnp.zeros((8, FF // 4), F32))
        start_square = whole_sum(start_square)

    def partial(send, i, value):
        send[i] = value.astype(BF)

    my_rows = rows_of(me.x, TQ)

    def products(p, send):
        for q in range(2):
            unpack_half(me.half, near_r.at[p, q], parts.at[q, 2 * p], parts.at[q, 2 * p + 1])
            for i in range(2):
                partial(send, 2 * q + i, nn(x[...], parts[q, 2 * p + i]))

    def cross(p, send, slots):
        for i in range(2):
            cross_s[p, i] = add_x(send, slots, my_rows, 2 + i).astype(BF)
        return fl.start(cross_s.at[p], cross_r.at[p], sems_p.at[0, p], sems_p.at[1, p], me.partner())

    def joined(p, send, slots, i):
        return add_x(send, slots, my_rows, i) + cross_r[p, i].astype(F32)

    with jax.named_scope("forward"):
        blocks_landed(flights[0])
        flights.append(send_blocks(me, fl, out_w.at[2], full_r, sems_w, sems_l.at[2, 0]))
        products(0, send_a)
        c_a = scatter_x(me, fl, send_a, slots_a, sems_a)
        blocks_landed(flights[1])
        products(1, send_d)
        landed(c_a)
        cross_a = cross(0, send_a, slots_a)
        c_d = scatter_x(me, fl, send_d, slots_d, sems_d)
    with jax.named_scope("hidden"):
        landed([cross_a])
        gate_pre, up_pre = joined(0, send_a, slots_a, 0), joined(0, send_a, slots_a, 1)
        val, slope, curve = gelu_parts(gate_pre)
        slope_up = slope * up_pre
        hh[0, my_rows, :] = (val * up_pre).astype(BF)
        c_h0 = gather_x(me, fl, hh.at[0:1], sems_h.at[0])
        mm[0, my_rows, :] = slope_up
        mm[1, my_rows, :] = val
        own[0] = slope
        own[1] = up_pre * curve
        landed(c_d)
        cross_d = cross(1, send_d, slots_d)

    def transposed(i, s):
        for b in range(DB // 128):
            cols = slice(b * 128, (b + 1) * 128)
            start_t[i, :, cols] = s[cols, :].astype(F32).T.astype(BF)

    with jax.named_scope("starts"):
        blocks_landed(flights[2])
        for i in range(NF // 2):
            rows = slice(i * 2 * WR, (i + 1) * 2 * WR)
            unpack(full_r.at[2 * i], full_r.at[2 * i + 1], w_down, s_down, rows)

    def far(part):
        blocks = pl.ds(part * 4, 4)
        return fl.start(
            near_r.at[1, 1, blocks], far_r.at[blocks], sems_p.at[0, 2 + part], sems_p.at[1, 2 + part], me.partner()
        )

    def out_post(total, rows, lanes):
        return ((total - target[rows, lanes].astype(F32)) / float(TOK)).astype(BF)

    def dot_post(total, rows, lanes):
        return (total / float(TOK)).astype(BF)

    ch_o = Chunk(me, fl, acc_o, send_o, (o0, o1, o2, o3, o4, o5), whole_low, 640, whole_back, 512)
    ch_p = Chunk(me, fl, acc_p, send_p, (p0, p1, p2, p3, p4, p5), outer_low, 384, outer_low, 384)
    ch_s = Chunk(me, fl, acc_p, send_p, (s0, s1, s2, s3, s4, s5), inner_low, 256, inner_back, 128)
    with jax.named_scope("outputs"):
        landed(c_h0)
        ch_o.put(nt(hh[0], w_down[...]))
        ch_o.cores()
        landed([cross_d])
        gate_dot, up_dot = joined(1, send_d, slots_d, 0), joined(1, send_d, slots_d, 1)
        hh[1, my_rows, :] = (mm[0, my_rows, :] * gate_dot + mm[1, my_rows, :] * up_dot).astype(BF)
        c_h1 = gather_x(me, fl, hh.at[1:2], sems_h.at[1])
        own[2] = gate_dot
        own[3] = up_dot
        ch_o.ys()
        landed(c_h1)
        c_m = gather_x(me, fl, mm, sems_m)
        ch_p.put(nt(hh[1], w_down[...]) + nt(hh[0], s_down[...]))
        ch_p.cores()
        ch_s.cores()
        ch_o.zs()
        ch_p.ys()
        ch_s.ys()
        ch_o.reduce(go, out_post)
        ch_p.zs()
        ch_s.zs()
        ch_o.spread()
        ch_p.reduce(gd, dot_post)
        ch_s.reduce(gd, dot_post)
        ch_o.collect()
    with jax.named_scope("back"):
        partial(send_b, 0, nn(go[...], w_down[...]))
        c_b = scatter_x(me, fl, send_b, slots_b, sems_b)
        c_far = [far(0)]
        ch_p.spread()
        ch_s.spread()
        ch_p.collect()
        ch_s.collect()
        partial(send_c, 0, nn(gd[...], w_down[...]) + nn(go[...], s_down[...]))
        c_c = scatter_x(me, fl, send_c, slots_c, sems_c)
        image = tn(hh[1], go[...]) + tn(hh[0], gd[...])
        one[2] = image
        u1d[...] = image.astype(BF)
        transposed(2, s_down)
        landed(c_b)
        grad_hidden = add_x(send_b, slots_b, my_rows, 0)
        own[0] = grad_hidden * own[0]
        own[1] = grad_hidden * own[1]
        landed(c_c)
        back_dot = add_x(send_c, slots_c, my_rows, 0)
        slope_term, curve_term = own[0], own[1]
        gu1[0, my_rows, :] = (
            back_dot * mm[0, my_rows, :] + slope_term * own[3] + curve_term * own[2]
        ).astype(BF)
        gu1[1, my_rows, :] = (back_dot * mm[1, my_rows, :] + slope_term * own[2]).astype(BF)
        c_g1 = gather_x(me, fl, gu1, sems_g1)
        landed(c_m)
        landed(c_k)
        total = kp[...] + (kr[0] + kr[1] + kr[2])
        high = total.astype(BF)
        kpair[0] = high
        kpair[1] = (total - high.astype(F32)).astype(BF)
        landed(c_g1)

    with jax.named_scope("second"):
        for i in range(2):
            tan2[i] = nn(kpair[0], gu1[i]) + nn(kpair[1], gu1[i])
        h2[...] = (mm[0] * tan2[0] + mm[1] * tan2[1]).astype(BF)
        ch_q = Chunk(me, fl, acc_o, send_o, (q0, q1, q2, q3, q4, q5), outer_low, 384, outer_low, 384)
        ch_r = Chunk(me, fl, acc_o, send_o, (r0, r1, r2, r3, r4, r5), inner_low, 256, inner_back, 128)
        for copy in ch_o.c1.values():
            copy.wait_send()
        done = [id(copy) for copy in ch_o.c1.values()]
        fl.sent = [copy for copy in fl.sent if id(copy) not in done]
        ch_q.put(nt(h2[...], w_down[...]) + nn(hh[0], u1d[...]))
        ch_q.cores()
        ch_r.cores()
        ch_q.ys()
        ch_r.ys()

    def dots_one(b, carry):
        rows = rows_of(b, BLK)
        su, uu = carry
        s = start_t[2, rows, :].astype(F32) * SCALE
        u = one[2, rows, :] * SCALE
        return su + fold(s * u), uu + fold(u * u)

    zero = jnp.zeros((8, DB), F32)
    sum1 = ScalarSum(me, fl, sbuf1, ssem1)
    with jax.named_scope("image"):
        one[0] = tn(gu1[0], x[...])
        one[1] = tn(gu1[1], x[...])
        ch_q.zs()
        ch_r.zs()
        su, uu = lax.fori_loop(0, HB // BLK, dots_one, (zero, zero))
        su, uu = whole_sum(su), whole_sum(uu)
        for i in range(2):
            g = gu1[i, my_rows, :].astype(F32) * SCALE
            su = su + whole_sum(own[2 + i] * SCALE * g)
            uu = uu + whole_sum(tan2[i, my_rows, :] * SCALE * g)
        ch_q.reduce(g2, dot_post)
        ch_r.reduce(g2, dot_post)
        sum1.go(0, tile_of([start_square, su, uu]))
        ch_q.spread()
        ch_r.spread()
        sum1.go(1, sum1.get())
        ch_q.collect()
        ch_r.collect()

    with jax.named_scope("back_second"):
        partial(send_f, 0, nn(g2[...], w_down[...]) + nt(go[...], u1d[...]))
        c_f = scatter_x(me, fl, send_f, slots_f, sems_f)
        c_far.append(far(1))
        out_d[...] = tn(h2[...], go[...]) + tn(hh[0], g2[...])
        sum1.go(2, sum1.get())
        landed(c_f)
        back_dot = add_x(send_f, slots_f, my_rows, 0)
        gate_two = tan2[0, my_rows, :]
        up_two = tan2[1, my_rows, :]
        gu2[0, my_rows, :] = (
            back_dot * mm[0, my_rows, :] + own[0] * up_two + own[1] * gate_two
        ).astype(BF)
        gu2[1, my_rows, :] = (back_dot * mm[1, my_rows, :] + own[0] * gate_two).astype(BF)
        c_g2 = gather_x(me, fl, gu2, sems_g2)
        norms = sum1.get() * (1.0 / (SCALE * SCALE * ENTRIES))
    s_s, s_u, u_u = norms[0:1, 0:1], norms[1:2, 0:1], norms[2:3, 0:1]
    f = 1.0 / jnp.sqrt(s_s + EPS)
    v11 = f * f * s_s
    h11 = f * f * s_u
    w11 = f * f * u_u
    rr = jnp.maximum(w11 - h11 * h11 * (2.0 - v11), 0.0)
    h21 = jnp.sqrt(rr + EPS)
    v12 = (h11 - h11 * v11) / h21
    v22 = rr / (h21 * h21)
    a1 = f / h21
    a0 = -h11 * f / h21

    def dots_two(b, carry):
        rows = rows_of(b, BLK)
        p1, p2, pw = carry
        s = start_t[2, rows, :].astype(F32)
        u = one[2, rows, :]
        w = (a1 * out_d[rows, :] + a0 * u) * SCALE
        first = f * s * SCALE
        second = (a1 * u + a0 * s) * SCALE
        return p1 + fold(first * w), p2 + fold(second * w), pw + fold(w * w)

    with jax.named_scope("last_dots"):
        d1, d2, dw = lax.fori_loop(0, HB // BLK, dots_two, (zero, zero, zero))
        d1, d2, dw = whole_sum(d1), whole_sum(d2), whole_sum(dw)
        for i in range(2):
            w = (
                a1 * gu2[i, my_rows, :].astype(F32) + a0 * gu1[i, my_rows, :].astype(F32)
            ) * SCALE
            first = own[2 + i]
            second = a1 * tan2[i, my_rows, :] + a0 * first
            d1 = d1 + whole_sum((f * SCALE) * first * w)
            d2 = d2 + whole_sum(second * SCALE * w)
        sum2 = ScalarSum(me, fl, sbuf2, ssem2)
        sum2.go(0, tile_of([d1, d2, dw]))
        landed(c_g2)
        dw = jnp.zeros((1, 1), F32)
        for i in range(2):
            w = (a1 * gu2[i].astype(F32) + a0 * gu1[i].astype(F32)) * SCALE
            high = w.astype(BF)
            low = (w - high.astype(F32)).astype(BF)
            kw = nn(kpair[0], high) + nn(kpair[1], high) + nn(kpair[0], low)
            dw = dw + whole_sum(w * kw)
        blank = jnp.zeros((1, 1), F32)
        sum2.go(1, sum2.get() + tile_of([blank, blank, dw]))
        out_g[...] = tn(gu2[0], x[...])
        sum2.go(2, sum2.get())
        out_u[...] = tn(gu2[1], x[...])
        landed(c_far)
        unpack_half(1 - me.half, far_r, parts.at[0, 2], parts.at[0, 3])
        transposed(0, parts.at[0, 2])
        transposed(1, parts.at[0, 3])
        norms = sum2.get() * (1.0 / (SCALE * SCALE * ENTRIES))
    h12, h22, ww = norms[0:1, 0:1], norms[1:2, 0:1], norms[2:3, 0:1]
    rr = (
        ww
        - 2.0 * (h12 * h12 + h22 * h22)
        + h12 * h12 * v11
        + h22 * h22 * v22
        + 2.0 * h12 * h22 * v12
    )
    h32 = jnp.sqrt(jnp.maximum(rr, 0.0) + EPS)
    c2 = a1 / h32
    c1 = (a0 - h22 * a1) / h32
    c0 = -(h12 * f + h22 * a0) / h32
    for i, value in enumerate((h21, h12, h22, h32)):
        hess[i] = jnp.max(value)
    ray[0] = jnp.max(h11)

    def third(b, carry):
        rows = rows_of(b, BLK)
        for i in range(3):
            twos[i][rows, :] = (
                c2 * twos[i][rows, :] + c1 * one[i, rows, :] + c0 * start_t[i, rows, :].astype(F32)
            )
        return carry

    with jax.named_scope("third"):
        lax.fori_loop(0, HB // BLK, third, 0)

    for copy in fl.sent:
        copy.wait_send()
    for chunk in (ch_o, ch_p, ch_s, ch_q, ch_r):
        chunk.drain()


def rounds(*operands):
    dma = pltpu.SemaphoreType.DMA

    def xround(n):
        return [pltpu.VMEM((n, TOK, HB), BF), pltpu.VMEM((3, n, TQ, HB), BF), dma((2, 3))]

    scratch = (
        [pltpu.VMEM((3, NF, BR, WL), BF), pltpu.VMEM((2, 2, 8, BR, WL), BF), pltpu.VMEM((NF, BR, WL), BF), pltpu.VMEM((8, BR, WL), BF)]
        + [dma((2, NF)), dma((2, 2, 2, 8)), dma((3, 2)), dma((2, 4))]
        + [pltpu.VMEM((2, 4, DB, HB), BF)] + [pltpu.VMEM((DB, HB), BF)] * 2
        + [pltpu.VMEM((3, HB, DB), BF), pltpu.VMEM((3, HB, DB), F32)] + [pltpu.VMEM((2, 2, TQ, HB), BF)] * 2
        + [pltpu.VMEM((TOK, TOK), F32), pltpu.VMEM((3, TOK, TOK), F32), pltpu.VMEM((2, TOK, TOK), BF), dma((2, 3))]
        + xround(4) + xround(4)
        + [pltpu.VMEM((4, TQ, HB), F32), pltpu.VMEM((2, TOK, HB), BF), dma((2, 2, 3)), pltpu.VMEM((2, TOK, HB), F32), dma((2, 3))]
        + [pltpu.VMEM((TOK, DB), F32), pltpu.VMEM((TOK, DB), BF)] * 2
        + chunk_scratch(640) + chunk_scratch(384) + chunk_scratch(256)
        + [pltpu.VMEM((TOK, DB), BF)] * 2
        + xround(1) + xround(1)
        + [pltpu.VMEM((2, TOK, HB), BF), dma((2, 3)), pltpu.VMEM((HB, DB), BF), pltpu.VMEM((2, TOK, HB), F32), pltpu.VMEM((TOK, HB), BF)]
        + chunk_scratch(384) + chunk_scratch(256)
        + [pltpu.VMEM((TOK, DB), BF)]
        + xround(1)
        + [pltpu.VMEM((2, TOK, HB), BF), dma((2, 3))]
        + [pltpu.VMEM((24, 8, 128), F32), dma((2, 24)), pltpu.VMEM((24, 8, 128), F32), dma((2, 24))]
    )
    wide = jax.ShapeDtypeStruct((HB, DB), F32)
    return pl.pallas_call(
        kernel,
        out_shape=(wide, wide, wide, jax.ShapeDtypeStruct((4,), F32), jax.ShapeDtypeStruct((1,), F32)),
        in_specs=[pl.BlockSpec(memory_space=pltpu.VMEM)] * 8,
        out_specs=[pl.BlockSpec(memory_space=pltpu.VMEM)] * 3 + [pl.BlockSpec(memory_space=pltpu.SMEM)] * 2,
        scratch_shapes=scratch,
        compiler_params=pltpu.CompilerParams(
            collective_id=0, has_side_effects=True, vmem_limit_bytes=60 * 1024 * 1024
        ),
        name="arnoldi",
    )(*operands)


def on_device(inputs, target, w_gate, w_up, w_down, start_gate, start_up, start_down):
    third_g, third_u, third_d, hess, ray = rounds(
        inputs, target, w_gate, w_up, w_down.T, start_gate, start_up, start_down.T
    )
    return (
        third_g.T.reshape(DB, 1, HB),
        third_u.T.reshape(DB, 1, HB),
        third_d.reshape(1, HB, DB),
        hess,
        ray,
    )


def solution(mesh):
    placed = (
        P(None, "dcn"),
        P(None, "dcn"),
        P(("dcn", "fsdp"), "tp"),
        P(("dcn", "fsdp"), "tp"),
        P("tp", ("dcn", "fsdp")),
        P(("dcn", "fsdp"), "tp"),
        P(("dcn", "fsdp"), "tp"),
        P("tp", ("dcn", "fsdp")),
    )
    return jax.shard_map(
        on_device,
        mesh=mesh,
        in_specs=placed,
        out_specs=(
            P("dcn", "tp", "fsdp"),
            P("dcn", "tp", "fsdp"),
            P("tp", "fsdp", "dcn"),
            P(),
            P(),
        ),
        check_vma=False,
    )
```
